128 devices in a mesh: dp: 4 (over x), row: 2 (over core), col: 16 (over z, y).
Axes of the slice: x: 4, y: 4, z: 4, core: 2. Of those that a mesh axis runs over, the one named last changes fastest.
Arguments:
- hidden_in: bfloat16 [8192, 1024], P(('dp', 'col'), 'row'), may hold values from -6 to 6
- segment_ids: int32 [4, 2048], P('dp'), may hold values from 0 to 3, never falling along the last dimension, each value on 1 to 1024 neighbouring positions
- first_gain: float32 [1024], P('row'), may hold values from 0.25 to 1.75
- mixer_b: bfloat16 [1024, 1024], P('row', 'col'), may hold values from -0.1875 to 0.1875
- mixer_c: bfloat16 [1024, 1024], P('row', 'col'), may hold values from -0.1875 to 0.1875
- mixer_v: bfloat16 [1024, 1024], P('row', 'col'), may hold values from -0.1875 to 0.1875
- conv_kernel: float32 [3, 1024], P(None, 'col'), may hold values from -3 to 3
- mixer_out: bfloat16 [1024, 1024], P('col', 'row'), may hold values from -0.1875 to 0.1875
- second_gain: float32 [1024], P('row'), may hold values from 0.25 to 1.75
- gate_weight: bfloat16 [1024, 4608], P('row', 'col'), may hold values from -0.1875 to 0.1875
- up_weight: bfloat16 [1024, 4608], P('row', 'col'), may hold values from -0.1875 to 0.1875
- down_weight: bfloat16 [4608, 1024], P('col', 'row'), may hold values from -0.09375 to 0.09375
- cotangent: bfloat16 [8192, 1024], P(('dp', 'col'), 'row'), may hold values from -6 to 6
Outputs:
- block_out: bfloat16 [8192, 1024], P(('dp', 'col'), 'row')
- input_grad: float32 [8192, 1024], P(('dp', 'col'), 'row')
- first_gain_grad: float32 [1024], P('row')
- mixer_b_grad: float32 [1024, 1024], P('row', 'col')
- mixer_c_grad: float32 [1024, 1024], P('row', 'col')
- mixer_v_grad: float32 [1024, 1024], P('row', 'col')
- kernel_grad: float32 [3, 1024], P(None, ('col', 'row'))
- mixer_out_grad: float32 [1024, 1024], P('col', 'row')
- second_gain_grad: float32 [1024], P('row')
- gate_grad: float32 [1024, 4608], P('row', 'col')
- up_grad: float32 [1024, 4608], P('row', 'col')
- down_grad: float32 [4608, 1024], P('col', 'row')
The draws below stay inside these ranges and needn't reach their ends.
Inputs may be any that keep to these rules, and one draw needn't show every extreme that they name: `segment_ids`: within each sequence the ids never fall; each of the 4 documents of a sequence has 1 to 1024 tokens, and one has exactly that many.
All inputs are finite; a program needn't handle non-finite values.
Results may differ from the reference program's by a relative error of at most 0.0096.
Values may be sent and summed in bfloat16 or wider, within the bound.
A program may use at most 128 MiB of HBM per device.

```python
import math
import jax
import jax.numpy as jnp
import numpy as np
from jax import lax

D = 1024
FF = 4608
KW = 3
SEQ_LEN = 2048
DOCS = 4
NSEQ = 4
TOKENS = 8192


def steps_of(rng, shape, cuts, least, largest):
    gain = 1.0
    for axis_at, blocks in cuts:
        steps = jax.random.uniform(jax.random.fold_in(jax.random.fold_in(rng, 6), axis_at), (blocks,), jnp.float32, least / len(cuts), largest / len(cuts))
        gain = gain * jnp.repeat(jnp.exp(steps), shape[axis_at] // blocks).reshape((-1,) + (1,) * (len(shape) - 1 - axis_at))
    return gain


def length_profile(amount, total, bound, skew):
    loads = [(1 << 20) // math.isqrt(rank ** skew) + 1 for rank in range(2, amount + 1)]
    spare, given = total - bound - (amount - 1), [1] * (amount - 1)
    while spare > 0:
        movable = [i for i in range(amount - 1) if given[i] < bound]
        whole, left = sum([loads[i] for i in movable]), spare
        for i in movable:
            more = min(bound - given[i], max(1, left * loads[i] // whole), spare)
            given[i] = given[i] + more
            spare = spare - more
    return np.array([bound] + given)


def ragged_sizes(own_key, count, total, limit, skew):
    if count == 2:
        one = jax.random.randint(own_key, (), max(1, total - limit), min(limit, total - 1) + 1)
        return jnp.stack([one, total - one])
    sizes = jnp.asarray(length_profile(count, total, limit, skew), jnp.int32)
    pairs = (count - 1) // 2
    donor, receiver = sizes[1:1 + 2 * pairs:2], sizes[2:2 + 2 * pairs:2]
    margin = jnp.minimum(donor - 1, limit - receiver)
    moved = jax.random.randint(jax.random.fold_in(own_key, 1), (pairs,), 0, 1 << 20) % (margin + 1)
    sizes = sizes.at[1:1 + 2 * pairs:2].set(donor - moved).at[2:2 + 2 * pairs:2].set(receiver + moved)
    return sizes[jax.random.permutation(jax.random.fold_in(own_key, 2), count)]


def noise(key, extent, spread, bound, split=(), held_as=jnp.bfloat16):
    array = spread * jax.random.normal(key, extent, jnp.float32)
    if split:
        array = array * steps_of(key, extent, split, -0.22, 0.18)
    return jnp.clip(array, -bound, bound).astype(held_as)


def setup_inputs(seed: int = 0) -> dict:
    streams_of = jax.random.split(jax.random.key(seed), 14)
    return {
        "hidden_in": noise(streams_of[0], (TOKENS, D), 1.0, 6.0, ((0, 64), (1, 2))),
        "segment_ids": jax.vmap(lambda own: jnp.searchsorted(jnp.cumsum(ragged_sizes(own, DOCS, SEQ_LEN, SEQ_LEN // 2, 1)), jnp.arange(SEQ_LEN), side="right"))(jax.random.split(streams_of[1], NSEQ)).reshape((NSEQ, SEQ_LEN)).astype(jnp.int32),
        "first_gain": jnp.clip(1.0 + 0.15 * jax.random.normal(streams_of[2], (D,), jnp.float32), 0.25, 1.75),
        "mixer_b": noise(streams_of[3], (D, D), D ** -0.5, 0.1875, ((0, 2), (1, 16))),
        "mixer_c": noise(streams_of[4], (D, D), D ** -0.5, 0.1875, ((0, 2), (1, 16))),
        "mixer_v": noise(streams_of[5], (D, D), D ** -0.5, 0.1875, ((0, 2), (1, 16))),
        "conv_kernel": noise(streams_of[6], (KW, D), 0.6, 3.0, ((1, 16),), jnp.float32),
        "mixer_out": noise(streams_of[7], (D, D), D ** -0.5, 0.1875, ((0, 16), (1, 2))),
        "second_gain": jnp.clip(1.0 + 0.15 * jax.random.normal(streams_of[8], (D,), jnp.float32), 0.25, 1.75),
        "gate_weight": noise(streams_of[9], (D, FF), D ** -0.5, 0.1875, ((0, 2), (1, 16))),
        "up_weight": noise(streams_of[10], (D, FF), D ** -0.5, 0.1875, ((0, 2), (1, 16))),
        "down_weight": noise(streams_of[11], (FF, D), FF ** -0.5, 0.09375, ((0, 16), (1, 2))),
        "cotangent": noise(streams_of[12], (TOKENS, D), 1.0, 6.0, ((0, 64), (1, 2))),
    }


EPSILON = 1e-05

def delayed(values, offset):
    if offset == 0:
        return values
    filler = jnp.zeros((offset, values.shape[1]), values.dtype)
    return jnp.concatenate([filler, values[:-offset]], 0)

def advanced(values, offset):
    if offset == 0:
        return values
    filler = jnp.zeros((offset, values.shape[1]), values.dtype)
    return jnp.concatenate([values[offset:], filler], 0)

def boundary(segment_row, offset):
    current = segment_row.astype(jnp.int32)
    prior = jnp.concatenate([jnp.full((offset,), -1, jnp.int32), current[:current.shape[0] - offset]], 0)
    return (prior == current).astype(jnp.float32)[:, None]

def reference(hidden_in, segment_ids, first_gain, mixer_b, mixer_c, mixer_v, conv_kernel, mixer_out, second_gain, gate_weight, up_weight, down_weight, cotangent):
    features = hidden_in.shape[1]
    taps = conv_kernel.shape[0]
    sequences, seq_len = segment_ids.shape
    f32 = jnp.float32
    bf16 = jnp.bfloat16

    def one_sequence(totals, pieces):
        tokens_half, segment_row, cot_half = pieces
        x_float = tokens_half.astype(f32)
        first_scale = lax.rsqrt(lax.optimization_barrier(jnp.mean(x_float * x_float, axis=1, keepdims=True)) + EPSILON)
        first_normed = (x_float * first_scale * first_gain).astype(bf16)
        in_gate = jnp.dot(first_normed, mixer_b, preferred_element_type=f32)
        out_gate = jnp.dot(first_normed, mixer_c, preferred_element_type=f32)
        values = jnp.dot(first_normed, mixer_v, preferred_element_type=f32)
        gated_in = in_gate * values
        masks = [boundary(segment_row, offset) for offset in range(taps)]
        convolved = jnp.zeros_like(gated_in)
        for offset in range(taps):
            convolved = convolved + conv_kernel[offset][None, :] * masks[offset] * delayed(gated_in, offset)
        mixed = (out_gate * convolved).astype(bf16)
        residual = x_float + jnp.dot(mixed, mixer_out, preferred_element_type=f32)
        second_scale = lax.rsqrt(lax.optimization_barrier(jnp.mean(residual * residual, axis=1, keepdims=True)) + EPSILON)
        second_normed = (residual * second_scale * second_gain).astype(bf16)
        gate_pre = jnp.dot(second_normed, gate_weight, preferred_element_type=f32)
        up_pre = jnp.dot(second_normed, up_weight, preferred_element_type=f32)
        sigmoid_gate = jax.nn.sigmoid(gate_pre)
        silu_gate = gate_pre * sigmoid_gate
        hidden = (silu_gate * up_pre).astype(bf16)
        block_out = (residual + jnp.dot(hidden, down_weight, preferred_element_type=f32)).astype(bf16)
        down_grad = jnp.dot(hidden.T, cot_half, preferred_element_type=f32)
        hidden_grad = jnp.dot(cot_half, down_weight.T, preferred_element_type=f32)
        gate_delta = (hidden_grad * up_pre * sigmoid_gate * (1.0 + gate_pre * (1.0 - sigmoid_gate))).astype(bf16)
        up_delta = (hidden_grad * silu_gate).astype(bf16)
        gate_grad = jnp.dot(second_normed.T, gate_delta, preferred_element_type=f32)
        up_grad = jnp.dot(second_normed.T, up_delta, preferred_element_type=f32)
        second_grad = jnp.dot(gate_delta, gate_weight.T, preferred_element_type=f32) + jnp.dot(up_delta, up_weight.T, preferred_element_type=f32)
        second_gain_grad = lax.optimization_barrier(jnp.sum(second_grad * residual * second_scale, axis=0))
        second_weighted = second_grad * second_gain
        cube_two = second_scale * second_scale * second_scale
        residual_grad = cot_half.astype(f32) + second_scale * second_weighted - residual * cube_two * lax.optimization_barrier(jnp.mean(second_weighted * residual, axis=1, keepdims=True))
        residual_half = residual_grad.astype(bf16)
        mixer_out_grad = jnp.dot(mixed.T, residual_half, preferred_element_type=f32)
        mixed_grad = jnp.dot(residual_half, mixer_out.T, preferred_element_type=f32)
        out_gate_delta = (mixed_grad * convolved).astype(bf16)
        conv_grad = mixed_grad * out_gate
        kernel_rows = []
        gated_grad = jnp.zeros_like(conv_grad)
        for offset in range(taps):
            weighted = conv_grad * masks[offset]
            kernel_rows.append(lax.optimization_barrier(jnp.sum(weighted * delayed(gated_in, offset), axis=0)))
            gated_grad = gated_grad + advanced(weighted, offset) * conv_kernel[offset][None, :]
        kernel_grad = jnp.stack(kernel_rows, 0)
        in_gate_delta = (gated_grad * values).astype(bf16)
        values_delta = (gated_grad * in_gate).astype(bf16)
        mixer_b_grad = jnp.dot(first_normed.T, in_gate_delta, preferred_element_type=f32)
        mixer_c_grad = jnp.dot(first_normed.T, out_gate_delta, preferred_element_type=f32)
        mixer_v_grad = jnp.dot(first_normed.T, values_delta, preferred_element_type=f32)
        first_grad = jnp.dot(in_gate_delta, mixer_b.T, preferred_element_type=f32) + jnp.dot(out_gate_delta, mixer_c.T, preferred_element_type=f32) + jnp.dot(values_delta, mixer_v.T, preferred_element_type=f32)
        first_gain_grad = lax.optimization_barrier(jnp.sum(first_grad * x_float * first_scale, axis=0))
        first_weighted = first_grad * first_gain
        cube_one = first_scale * first_scale * first_scale
        input_grad = residual_grad + first_scale * first_weighted - x_float * cube_one * lax.optimization_barrier(jnp.mean(first_weighted * x_float, axis=1, keepdims=True))
        terms = (first_gain_grad, mixer_b_grad, mixer_c_grad, mixer_v_grad, kernel_grad, mixer_out_grad, second_gain_grad, gate_grad, up_grad, down_grad)
        new_totals = tuple((total + term for total, term in zip(totals, terms)))
        return (new_totals, (block_out, input_grad))
    start = (jnp.zeros((features,), f32), jnp.zeros(mixer_b.shape, f32), jnp.zeros(mixer_c.shape, f32), jnp.zeros(mixer_v.shape, f32), jnp.zeros(conv_kernel.shape, f32), jnp.zeros(mixer_out.shape, f32), jnp.zeros((features,), f32), jnp.zeros(gate_weight.shape, f32), jnp.zeros(up_weight.shape, f32), jnp.zeros(down_weight.shape, f32))
    totals, (outputs, input_grads) = lax.scan(one_sequence, start, (hidden_in.reshape(sequences, seq_len, features), segment_ids, cotangent.reshape(sequences, seq_len, features)))
    return (outputs.reshape(sequences * seq_len, features), input_grads.reshape(sequences * seq_len, features), totals[0], totals[1], totals[2], totals[3], totals[4], totals[5], totals[6], totals[7], totals[8], totals[9])
```

```python
import jax
import jax.numpy as jnp
from jax import lax
from jax.experimental import pallas as pl
from jax.experimental.pallas import tpu as pltpu
from jax.sharding import PartitionSpec as P

EPSILON = 1e-05
MESH = pl.DeviceIdType.MESH
F32 = jnp.float32
BF16 = jnp.bfloat16

D = 1024
HALF = 512
CH = 256
CB = 64
FQ = 1152
FB = 288
TC = 256
TO = 64
COPIES = 160


def mod4(value):
    return lax.rem(value + 4, 4)


def nt(a, b):
    return lax.dot_general(a, b, (((1,), (1,)), ((), ())), preferred_element_type=F32)


def nn(a, b):
    return lax.dot_general(a, b, (((1,), (0,)), ((), ())), preferred_element_type=F32)


def tn(a, b):
    return lax.dot_general(a, b, (((0,), (0,)), ((), ())), preferred_element_type=F32)


def loop(count, body):
    def step(i, carry):
        body(i)
        return carry

    lax.fori_loop(0, count, step, 0)


def rows_at(start, size, multiple=32):
    return pl.ds(pl.multiple_of(start, multiple), size)


def lanes_at(start, size):
    return pl.ds(pl.multiple_of(start, 128), size)


def kernel(
    x_in,
    cot_in,
    masks,
    small,
    mix_in,
    gate_in,
    up_in,
    down_in,
    block_o,
    input_o,
    mix_o,
    feed_o,
    stats_o,
    xs,
    cs,
    gains,
    taps_in,
    w_mix,
    w_feed,
    fn,
    pre,
    gat,
    cvd,
    mx,
    res,
    sn,
    gu,
    hid,
    dg,
    fulls,
    halves,
    recvs,
    rg,
    rh,
    cg,
    dm,
    go_f,
    cr_f,
    s_f,
    zr_f,
    xs_f,
    xr_f,
    xf_f,
    go_m,
    cr_m,
    s_m,
    zr_m,
    xs_m,
    xr_m,
    xf_m,
    st,
    st_y,
    st_z,
    st_x,
    bo_own,
    ig_own,
    ss,
    rs,
    ls,
):
    x = lax.axis_index("dp")
    r = lax.axis_index("row")
    col = lax.axis_index("col")
    z = lax.div(col, 4)
    y = lax.rem(col, 4)
    other = 1 - r
    own_lanes = lanes_at(r * HALF, HALF)
    other_lanes = lanes_at(other * HALF, HALF)
    own_rows = rows_at(y * TO, TO)

    def y_peer(d):
        return (x, r, z * 4 + mod4(y + d))

    def z_peer(d):
        return (x, r, mod4(z + d) * 4 + y)

    def x_peer(d):
        return (mod4(x + d), r, col)

    partner = (x, other, col)
    successor = (x, other, mod4(z + r) * 4 + y)
    predecessor = (x, other, mod4(z + r + 3) * 4 + y)
    halo_extra = (x, other, mod4(z + 2 * r - 1) * 4 + y)

    barrier = pltpu.get_barrier_semaphore()
    greeted = [partner, halo_extra]
    for d in (1, 2, 3):
        greeted += [y_peer(d), (x, other, z * 4 + mod4(y + d)), z_peer(d), x_peer(d)]
    for device in greeted:
        pl.semaphore_signal(barrier, inc=1, device_id=device, device_id_type=MESH)
    pl.semaphore_wait(barrier, len(greeted))

    used = [0]
    sent = []

    def slot(count=1):
        first = used[0]
        used[0] += count
        return first

    def push(source, target, device, index=None):
        i = slot() if index is None else index
        copy = pltpu.make_async_remote_copy(
            src_ref=source,
            dst_ref=target,
            send_sem=ss.at[i],
            recv_sem=rs.at[i],
            device_id=device,
            device_id_type=MESH,
        )
        copy.start()
        sent.append((None, copy))
        return copy

    def place(source, target, device, send_index, recv_index, here):
        copy = pltpu.make_async_remote_copy(
            src_ref=source,
            dst_ref=target,
            send_sem=ss.at[send_index],
            recv_sem=rs.at[recv_index],
            device_id=device,
            device_id_type=MESH,
        )

        @pl.when(here)
        def _():
            pltpu.make_async_copy(source, target, rs.at[recv_index]).start()

        @pl.when(jnp.logical_not(here))
        def _():
            copy.start()

        sent.append((here, copy))

    def arrived(source, target, index):
        pltpu.make_async_remote_copy(
            src_ref=source,
            dst_ref=target,
            send_sem=ss.at[index],
            recv_sem=rs.at[index],
            device_id=partner,
            device_id_type=MESH,
        ).wait_recv()

    def tokens_start(source, target):
        base = slot(4)
        core = lax.div(y, 2)
        block = lax.rem(y, 2)
        region = target.at[rows_at(block * 128, 128), own_lanes]
        for d in (1, 3, 2, 0):
            device = (x, core, z * 4 + mod4(y + d))
            index = base + block * 2 + r
            if d:
                copy = pltpu.make_async_remote_copy(
                    src_ref=source,
                    dst_ref=region,
                    send_sem=ss.at[base + d],
                    recv_sem=rs.at[index],
                    device_id=device,
                    device_id_type=MESH,
                )
                copy.start()
                sent.append((None, copy))
            else:
                place(source, region, device, base, index, core == r)
        return base

    def tokens_finish(source, target, base):
        for s in range(4):
            region = target.at[pl.ds((s // 2) * 128, 128), pl.ds((s % 2) * HALF, HALF)]
            arrived(source, region, base + s)

    def owners_start(source, target):
        base = slot(2)
        chip = 2 * r + lax.div(y, 2)
        region = target.at[rows_at(lax.rem(y, 2) * TO, TO)]
        for core in range(2):
            here = jnp.logical_and(chip == y, r == core)
            place(
                source.at[:, pl.ds(core * HALF, HALF)],
                region,
                (x, core, z * 4 + chip),
                base + core,
                base + lax.rem(y, 2),
                here,
            )
        return base

    def owners_finish(source, target, base):
        for s in range(2):
            arrived(source.at[:, pl.ds(0, HALF)], target.at[pl.ds(s * TO, TO)], base + s)

    local = [0]

    class Section:
        def __init__(self, source, region):
            self.source = source
            self.region = region

        def start(self):
            self.z = {d: push(self.source, self.region(z, r), z_peer(d)) for d in (1, 3, 2)}
            self.mine = pltpu.make_async_copy(self.source, self.region(z, r), ls.at[local[0]])
            local[0] += 1
            self.mine.start()
            self.cross = [push(self.source, self.region(z, r), partner)]

        def forward(self):
            for d in (1, 3, 2):
                self.z[d].wait_recv()
                region = self.region(mod4(z - d), r)
                self.cross.append(push(region, region, partner))

        def finish(self):
            self.mine.wait()
            for copy in self.cross:
                copy.wait_recv()

    mix = Section(
        mix_in, lambda zz, rr: w_mix.at[:, rows_at(zz * CB, CB), lanes_at(rr * HALF, HALF)]
    )
    gate = Section(
        gate_in, lambda zz, rr: w_feed.at[rows_at(zz * FB, FB), lanes_at(rr * HALF, HALF)]
    )
    up = Section(
        up_in, lambda zz, rr: w_feed.at[rows_at(FQ + zz * FB, FB), lanes_at(rr * HALF, HALF)]
    )
    down = Section(
        down_in,
        lambda zz, rr: w_feed.at[rows_at(2 * FQ + zz * FB, FB), lanes_at(rr * HALF, HALF)],
    )

    def scatter_start(k):
        return [
            push(halves.at[k, rows_at(mod4(y + d) * TO, TO)], recvs.at[k, d - 1], y_peer(d))
            for d in (1, 3, 2)
        ]

    def scatter_finish(k, copies):
        for copy in copies:
            copy.wait_recv()
        total = fulls[k, own_rows, :]
        for d in range(3):
            total = total + recvs[k, d].astype(F32)
        return total

    def gather_start(buffer):
        return [push(buffer.at[own_rows], buffer.at[own_rows], y_peer(d)) for d in (1, 3, 2)]

    def wait(copies):
        for copy in copies:
            copy.wait_recv()

    def product(k, value):
        def body(n):
            lanes = lanes_at(n * 256, 256)
            part = value(lanes)
            fulls[k, :, lanes] = part
            halves[k, :, lanes] = part.astype(BF16)

        loop(4, body)

    x_base = tokens_start(x_in, xs)
    mix.start()
    small_copies = [push(small, gains.at[:, own_lanes], partner)]
    small_copies += [push(small, taps_in.at[d - 1], z_peer(d)) for d in (1, 3, 2)]
    gains[:, own_lanes] = small[...]
    st[...] = jnp.zeros((8, D), F32)

    tokens_finish(x_in, xs, x_base)
    wait(small_copies)
    cot_base = tokens_start(cot_in, cs)
    first_gain = gains[0:1, :]
    second_gain = gains[1:2, :]
    taps = small[2:5, 0:CH]
    for d in range(3):
        taps = taps + taps_in[d, 2:5, 0:CH]

    def norm_body(i):
        rows = rows_at(i * 32, 32)
        value = xs[rows, :].astype(F32)
        scale = lax.rsqrt(jnp.sum(value * value, axis=1, keepdims=True) / D + EPSILON)
        fn[rows, :] = (value * scale * first_gain).astype(BF16)

    loop(8, norm_body)

    mix.forward()
    gate.start()
    up.start()
    mix.finish()

    def pre_body(s):
        pre[s] = nt(fn[...], w_mix[s])

    loop(3, pre_body)

    gat[8 : 8 + TC, :] = pre[0] * pre[2]
    halo = push(gat.at[pl.ds(TC, 8)], gat.at[pl.ds(0, 8)], successor)
    halo.wait_recv()
    m1 = masks[:, 0:1]
    m2 = masks[:, 1:2]
    cvd[...] = (
        taps[0:1] * gat[8 : 8 + TC, :]
        + taps[1:2] * (m1 * gat[7 : 7 + TC, :])
        + taps[2:3] * (m2 * gat[6 : 6 + TC, :])
    )
    mx[...] = (pre[1] * cvd[...]).astype(BF16)
    product(0, lambda lanes: nn(mx[...], w_mix[3, :, lanes]))
    first_scatter = scatter_start(0)

    residual = xs[own_rows, :].astype(F32) + scatter_finish(0, first_scatter)
    res[...] = residual
    second_scale = lax.rsqrt(jnp.sum(residual * residual, axis=1, keepdims=True) / D + EPSILON)
    sn[own_rows, :] = (residual * second_scale * second_gain).astype(BF16)
    sn_copies = gather_start(sn)

    gate.forward()
    up.forward()
    down.start()
    tokens_finish(cot_in, cs, cot_base)
    gate.finish()
    up.finish()
    wait(sn_copies)

    def gu_body(n):
        at = n * 256
        gu[:, lanes_at(at, 256)] = nt(sn[...], w_feed[rows_at(at, 256), :])

    loop(9, gu_body)

    down.forward()

    def hidden_body(i):
        rows = rows_at(i * 32, 32)
        g = gu[rows, 0:FQ]
        hid[rows, :] = (g * jax.nn.sigmoid(g) * gu[rows, FQ : 2 * FQ]).astype(BF16)

    loop(8, hidden_body)
    down.finish()

    def hg_body(n):
        at = n * 384
        gu[:, lanes_at(2 * FQ + at, 384)] = nt(cs[...], w_feed[rows_at(2 * FQ + at, 384), :])

    loop(3, hg_body)

    def delta_body(i):
        rows = rows_at(i * 32, 32)
        g = gu[rows, 0:FQ]
        u = gu[rows, FQ : 2 * FQ]
        hg = gu[rows, 2 * FQ : 3 * FQ]
        s = jax.nn.sigmoid(g)
        dg[rows, 0:FQ] = (hg * u * s * (1.0 + g * (1.0 - s))).astype(BF16)
        dg[rows, FQ : 2 * FQ] = (hg * (g * s)).astype(BF16)

    loop(8, delta_body)
    product(2, lambda lanes: nn(dg[...], w_feed[0 : 2 * FQ, lanes]))
    grad_scatter = scatter_start(2)
    product(1, lambda lanes: nn(hid[...], w_feed[2 * FQ : 3 * FQ, lanes]))
    block_scatter = scatter_start(1)

    def go_gu_body(n):
        at = n * 384
        go_f[rows_at(at, 384), :] = tn(dg[:, lanes_at(at, 384)], sn[:, other_lanes]).astype(BF16)

    def go_d_body(n):
        at = n * 384
        go_f[rows_at(2 * FQ + at, 384), :] = tn(
            hid[:, lanes_at(at, 384)], cs[:, other_lanes]
        ).astype(BF16)

    loop(6, go_gu_body)
    cross_gu = push(go_f.at[pl.ds(0, 2 * FQ)], cr_f.at[pl.ds(0, 2 * FQ)], partner)
    loop(3, go_d_body)
    cross_d = push(go_f.at[pl.ds(2 * FQ, FQ)], cr_f.at[pl.ds(2 * FQ, FQ)], partner)

    second_grad = scatter_finish(2, grad_scatter)
    residual = res[...]
    second_scale = lax.rsqrt(jnp.sum(residual * residual, axis=1, keepdims=True) / D + EPSILON)
    st[1:2, :] = jnp.sum(second_grad * residual * second_scale, axis=0, keepdims=True)
    weighted = second_grad * second_gain
    cube = second_scale * second_scale * second_scale
    residual_grad = (
        cs[own_rows, :].astype(F32)
        + second_scale * weighted
        - residual * cube * (jnp.sum(weighted * residual, axis=1, keepdims=True) / D)
    )
    rg[...] = residual_grad
    rh[own_rows, :] = residual_grad.astype(BF16)
    rh_copies = gather_start(rh)

    cross_gu.wait_recv()

    def s_gu_body(n):
        at = n * 384
        rows = rows_at(at, 384)
        s_f[rows, :] = (
            tn(dg[:, lanes_at(at, 384)], sn[:, own_lanes]) + cr_f[rows, :].astype(F32)
        ).astype(BF16)

    loop(6, s_gu_body)

    def feed_send(part):
        return [
            push(
                s_f.at[rows_at(part * FQ + mod4(z + d) * FB, FB)],
                zr_f.at[d - 1, pl.ds(part * FB, FB)],
                z_peer(d),
            )
            for d in (1, 3, 2)
        ]

    feed_z = feed_send(0) + feed_send(1)
    cross_d.wait_recv()

    def s_d_body(n):
        at = n * 384
        rows = rows_at(2 * FQ + at, 384)
        s_f[rows, :] = (
            tn(hid[:, lanes_at(at, 384)], cs[:, own_lanes]) + cr_f[rows, :].astype(F32)
        ).astype(BF16)

    loop(3, s_d_body)
    feed_z += feed_send(2)

    wait(rh_copies)
    mixed_grad = nt(rh[...], w_mix[3])
    cg[0:TC, :] = mixed_grad * pre[1]
    halo_back = push(cg.at[pl.ds(0, 8)], cg.at[pl.ds(TC, 8)], predecessor)
    dm[1] = (mixed_grad * cvd[...]).astype(BF16)

    def grad_rows(s, first, lanes):
        return tn(first, lanes)

    go_m[3] = tn(mx[...], rh[:, other_lanes]).astype(BF16)

    conv_grad = cg[0:TC, :]
    tap_lanes = lanes_at(y * CH, CH)
    st[2:3, tap_lanes] = jnp.sum(conv_grad * gat[8 : 8 + TC, :], axis=0, keepdims=True)
    st[3:4, tap_lanes] = jnp.sum(conv_grad * m1 * gat[7 : 7 + TC, :], axis=0, keepdims=True)
    st[4:5, tap_lanes] = jnp.sum(conv_grad * m2 * gat[6 : 6 + TC, :], axis=0, keepdims=True)
    halo_back.wait_recv()
    gated_grad = (
        taps[0:1] * conv_grad
        + taps[1:2] * (masks[:, 2:3] * cg[1 : 1 + TC, :])
        + taps[2:3] * (masks[:, 3:4] * cg[2 : 2 + TC, :])
    )
    dm[0] = (gated_grad * pre[2]).astype(BF16)
    dm[2] = (gated_grad * pre[0]).astype(BF16)

    def first_part(lanes):
        part = nn(dm[0], w_mix[0, :, lanes])
        part = part + nn(dm[1], w_mix[1, :, lanes])
        return part + nn(dm[2], w_mix[2, :, lanes])

    product(3, first_part)
    first_scatter = scatter_start(3)

    def go_m_body(s):
        go_m[s] = tn(dm[s], fn[:, other_lanes]).astype(BF16)

    loop(3, go_m_body)
    cross_m = push(go_m, cr_m, partner)

    bo_own[...] = (res[...] + scatter_finish(1, block_scatter)).astype(BF16)
    bo_base = owners_start(bo_own, block_o)

    cross_m.wait_recv()

    def s_m_body(s):
        s_m[s] = (tn(dm[s], fn[:, own_lanes]) + cr_m[s].astype(F32)).astype(BF16)

    loop(3, s_m_body)
    s_m[3] = (tn(mx[...], rh[:, own_lanes]) + cr_m[3].astype(F32)).astype(BF16)
    mix_z = [
        push(s_m.at[:, rows_at(mod4(z + d) * CB, CB), :], zr_m.at[d - 1], z_peer(d))
        for d in (1, 3, 2)
    ]

    wait(feed_z)
    for part in range(3):
        mine = s_f[rows_at(part * FQ + z * FB, FB), :].astype(F32)
        at = part * FB
        for d in range(3):
            mine = mine + zr_f[d, at : at + FB, :].astype(F32)
        xs_f[at : at + FB, :] = mine.astype(BF16)
    feed_x = [
        push(xs_f.at[:, lanes_at(mod4(x + d) * 128, 128)], xr_f.at[d - 1], x_peer(d))
        for d in (1, 3, 2)
    ]

    first_grad = scatter_finish(3, first_scatter)
    value = xs[own_rows, :].astype(F32)
    first_scale = lax.rsqrt(jnp.sum(value * value, axis=1, keepdims=True) / D + EPSILON)
    st[0:1, :] = jnp.sum(first_grad * value * first_scale, axis=0, keepdims=True)
    weighted = first_grad * first_gain
    cube = first_scale * first_scale * first_scale
    ig_own[...] = (
        rg[...]
        + first_scale * weighted
        - value * cube * (jnp.sum(weighted * value, axis=1, keepdims=True) / D)
    )
    ig_base = owners_start(ig_own, input_o)
    stat_copies = [push(st, st_y.at[0], partner)]
    for d in (1, 2, 3):
        stat_copies.append(push(st, st_y.at[2 * d - 1], y_peer(d)))
        stat_copies.append(push(st, st_y.at[2 * d], (x, other, z * 4 + mod4(y + d))))

    x_lanes = lanes_at(x * 128, 128)
    wait(feed_x)
    mine = xs_f[:, x_lanes].astype(F32)
    for d in range(3):
        mine = mine + xr_f[d].astype(F32)
    xf_f[:, x_lanes] = mine.astype(BF16)
    feed_g = [push(xf_f.at[:, x_lanes], xf_f.at[:, x_lanes], x_peer(d)) for d in (1, 3, 2)]

    wait(stat_copies)
    total = st[...]
    for i in range(7):
        total = total + st_y[i]
    st_z[3] = total
    stat_copies = [push(st_z.at[3], st_z.at[d - 1], z_peer(d)) for d in (1, 3, 2)]

    wait(mix_z)
    mine = s_m[:, rows_at(z * CB, CB), :].astype(F32)
    for d in range(3):
        mine = mine + zr_m[d].astype(F32)
    xs_m[...] = mine.astype(BF16)
    mix_x = [
        push(xs_m.at[:, :, lanes_at(mod4(x + d) * 128, 128)], xr_m.at[d - 1], x_peer(d))
        for d in (1, 3, 2)
    ]
    wait(stat_copies)
    st_x[3] = st_z[0] + st_z[1] + st_z[2] + st_z[3]
    stat_copies = [push(st_x.at[3], st_x.at[d - 1], x_peer(d)) for d in (1, 3, 2)]

    wait(mix_x)
    mine = xs_m[:, :, x_lanes].astype(F32)
    for d in range(3):
        mine = mine + xr_m[d].astype(F32)
    xf_m[:, :, x_lanes] = mine.astype(BF16)
    mix_g = [push(xf_m.at[:, :, x_lanes], xf_m.at[:, :, x_lanes], x_peer(d)) for d in (1, 3, 2)]

    wait(feed_g)
    feed_o[...] = xf_f[...].astype(F32)
    owners_finish(bo_own, block_o, bo_base)
    owners_finish(ig_own, input_o, ig_base)
    wait(stat_copies)
    stats_o[...] = st_x[0] + st_x[1] + st_x[2] + st_x[3]
    wait(mix_g)
    mix_o[...] = xf_m[...].astype(F32)

    for here, copy in sent:
        if here is None:
            copy.wait_send()
        else:

            @pl.when(jnp.logical_not(here))
            def _(copy=copy):
                copy.wait_send()


def shards(
    hidden_in,
    segment_ids,
    first_gain,
    mixer_b,
    mixer_c,
    mixer_v,
    conv_kernel,
    mixer_out,
    second_gain,
    gate_weight,
    up_weight,
    down_weight,
    cotangent,
):
    r = lax.axis_index("row")
    col = lax.axis_index("col")
    z = col // 4
    y = col % 4
    ids = segment_ids[0]
    length = ids.shape[0]
    outside = jnp.full((2,), -1, jnp.int32)
    padded = jnp.concatenate([outside, ids, outside - 1])
    m1 = padded[1 : 1 + length] == ids
    m2 = padded[:length] == ids
    n1 = padded[3 : 3 + length] == ids
    n2 = padded[4 : 4 + length] == ids
    masks = jnp.stack([m1, m2, n1, n2], 1).astype(F32)
    masks = lax.dynamic_slice_in_dim(masks, z * 512 + r * TC, TC, 0)
    masks = jnp.pad(masks, ((0, 0), (0, 124)))
    tap_rows = lax.dynamic_update_slice(jnp.zeros((3, HALF), F32), conv_kernel, (0, z * CB))
    small = jnp.concatenate(
        [first_gain[None], second_gain[None], tap_rows, jnp.zeros((3, HALF), F32)], 0
    )
    mix = jnp.stack([mixer_b.T, mixer_c.T, mixer_v.T, mixer_out], 0)
    vmem = pl.BlockSpec(memory_space=pltpu.VMEM)
    shape = jax.ShapeDtypeStruct
    scratch = [
        ((TC, D), BF16),
        ((TC, D), BF16),
        ((8, D), F32),
        ((3, 8, HALF), F32),
        ((4, CH, D), BF16),
        ((3 * FQ, D), BF16),
        ((TC, D), BF16),
        ((3, TC, CH), F32),
        ((TC + 8, CH), F32),
        ((TC, CH), F32),
        ((TC, CH), BF16),
        ((TO, D), F32),
        ((TC, D), BF16),
        ((TC, 3 * FQ), F32),
        ((TC, FQ), BF16),
        ((TC, 2 * FQ), BF16),
        ((4, TC, D), F32),
        ((4, TC, D), BF16),
        ((4, 3, TO, D), BF16),
        ((TO, D), F32),
        ((TC, D), BF16),
        ((TC + 8, CH), F32),
        ((3, TC, CH), BF16),
        ((3 * FQ, HALF), BF16),
        ((3 * FQ, HALF), BF16),
        ((3 * FQ, HALF), BF16),
        ((3, 3 * FB, HALF), BF16),
        ((3 * FB, HALF), BF16),
        ((3, 3 * FB, 128), BF16),
        ((3 * FB, HALF), BF16),
        ((4, CH, HALF), BF16),
        ((4, CH, HALF), BF16),
        ((4, CH, HALF), BF16),
        ((3, 4, CB, HALF), BF16),
        ((4, CB, HALF), BF16),
        ((3, 4, CB, 128), BF16),
        ((4, CB, HALF), BF16),
        ((8, D), F32),
        ((7, 8, D), F32),
        ((4, 8, D), F32),
        ((4, 8, D), F32),
        ((TO, D), BF16),
        ((TO, D), F32),
    ]
    block_out, input_grad, mix_grad, feed_grad, stats = pl.pallas_call(
        kernel,
        out_shape=(
            shape((128, HALF), BF16),
            shape((128, HALF), F32),
            shape((4, CB, HALF), F32),
            shape((3 * FB, HALF), F32),
            shape((8, D), F32),
        ),
        in_specs=[vmem] * 8,
        out_specs=(vmem,) * 5,
        scratch_shapes=[pltpu.VMEM(s, t) for s, t in scratch]
        + [
            pltpu.SemaphoreType.DMA((COPIES,)),
            pltpu.SemaphoreType.DMA((COPIES,)),
            pltpu.SemaphoreType.DMA((4,)),
        ],
        compiler_params=pltpu.CompilerParams(
            collective_id=0, has_side_effects=True, vmem_limit_bytes=62 * 2**20
        ),
    )(
        hidden_in,
        cotangent,
        masks,
        small,
        mix,
        gate_weight.T,
        up_weight.T,
        down_weight,
    )
    mine = lax.dynamic_slice_in_dim(stats[:2], r * HALF, HALF, 1)
    kernel_grad = lax.dynamic_slice(stats, (2, y * CH + z * CB + r * 32), (3, 32))
    return (
        block_out,
        input_grad,
        mine[0],
        mix_grad[0].T,
        mix_grad[1].T,
        mix_grad[2].T,
        kernel_grad,
        mix_grad[3],
        mine[1],
        feed_grad[:FB].T,
        feed_grad[FB : 2 * FB].T,
        feed_grad[2 * FB :],
    )


def solution(mesh):
    return jax.shard_map(
        shards,
        mesh=mesh,
        in_specs=(
            P(("dp", "col"), "row"),
            P("dp", None),
            P("row"),
            P("row", "col"),
            P("row", "col"),
            P("row", "col"),
            P(None, "col"),
            P("col", "row"),
            P("row"),
            P("row", "col"),
            P("row", "col"),
            P("col", "row"),
            P(("dp", "col"), "row"),
        ),
        out_specs=(
            P(("dp", "col"), "row"),
            P(("dp", "col"), "row"),
            P("row"),
            P("row", "col"),
            P("row", "col"),
            P("row", "col"),
            P(None, ("col", "row")),
            P("col", "row"),
            P("row"),
            P("row", "col"),
            P("row", "col"),
            P("col", "row"),
        ),
        check_vma=False,
    )
```

```python
import jax
import jax.numpy as jnp
from jax import lax
from jax.experimental import pallas as pl
from jax.experimental.pallas import tpu as pltpu
from jax.sharding import PartitionSpec as P

EPSILON = 1e-05
MESH = pl.DeviceIdType.MESH
F32 = jnp.float32
BF16 = jnp.bfloat16

D = 1024
HALF = 512
CH = 256
CB = 64
FQ = 1152
FB = 288
TC = 256
TO = 64
COPIES = 256


def mod4(value):
    return lax.rem(value + 4, 4)


def nt(a, b):
    return lax.dot_general(a, b, (((1,), (1,)), ((), ())), preferred_element_type=F32)


def nn(a, b):
    return lax.dot_general(a, b, (((1,), (0,)), ((), ())), preferred_element_type=F32)


def tn(a, b):
    return lax.dot_general(a, b, (((0,), (0,)), ((), ())), preferred_element_type=F32)


def loop(count, body):
    def step(i, carry):
        body(i)
        return carry

    lax.fori_loop(0, count, step, 0)


def rows_at(start, size, multiple=32):
    return pl.ds(pl.multiple_of(start, multiple), size)


def lanes_at(start, size):
    return pl.ds(pl.multiple_of(start, 128), size)


def kernel(
    x_in,
    cot_in,
    ids,
    first_in,
    second_in,
    taps_own,
    b_in,
    c_in,
    v_in,
    out_in,
    gate_in,
    up_in,
    down_in,
    block_o,
    input_o,
    b_o,
    c_o,
    v_o,
    out_o,
    gate_o,
    up_o,
    down_o,
    stats_o,
    small,
    masks,
    xs,
    cs,
    gains,
    taps_in,
    w_mix,
    w_feed,
    fn,
    pre,
    gat,
    cvd,
    mx,
    res,
    sn,
    gu,
    hid,
    dg,
    fulls,
    halves,
    recvs,
    rg,
    rh,
    cg,
    dm,
    go_f,
    cr_f,
    s_f,
    zr_f,
    xs_f,
    xr_f,
    xf_f,
    x1_d,
    t_d,
    z2_d,
    go_m,
    cr_m,
    s_m,
    zr_m,
    xs_m,
    xr_m,
    xf_m,
    x1_m,
    t_m,
    z2_m,
    st,
    st_y,
    st_z,
    st_x,
    bo_own,
    ig_own,
    ss,
    rs,
    ls,
):
    x = lax.axis_index("dp")
    r = lax.axis_index("row")
    col = lax.axis_index("col")
    z = lax.div(col, 4)
    y = lax.rem(col, 4)
    other = 1 - r
    own_lanes = lanes_at(r * HALF, HALF)
    other_lanes = lanes_at(other * HALF, HALF)
    own_rows = rows_at(y * TO, TO)

    def y_peer(d):
        return (x, r, z * 4 + mod4(y + d))

    def z_peer(d):
        return (x, r, mod4(z + d) * 4 + y)

    def x_peer(d):
        return (mod4(x + d), r, col)

    partner = (x, other, col)
    successor = (x, other, mod4(z + r) * 4 + y)
    predecessor = (x, other, mod4(z + r + 3) * 4 + y)
    halo_extra = (x, other, mod4(z + 2 * r - 1) * 4 + y)

    barrier = pltpu.get_barrier_semaphore()
    greeted = [partner, halo_extra]
    for d in (1, 2, 3):
        greeted += [y_peer(d), (x, other, z * 4 + mod4(y + d)), z_peer(d), x_peer(d)]
    for device in greeted:
        pl.semaphore_signal(barrier, inc=1, device_id=device, device_id_type=MESH)
    pl.semaphore_wait(barrier, len(greeted))

    used = [0]
    sent = []

    def slot(count=1):
        first = used[0]
        used[0] += count
        return first

    def push(source, target, device, index=None):
        i = slot() if index is None else index
        copy = pltpu.make_async_remote_copy(
            src_ref=source,
            dst_ref=target,
            send_sem=ss.at[i],
            recv_sem=rs.at[i],
            device_id=device,
            device_id_type=MESH,
        )
        copy.start()
        sent.append((None, copy))
        return copy

    def place(source, target, device, send_index, recv_index, here):
        copy = pltpu.make_async_remote_copy(
            src_ref=source,
            dst_ref=target,
            send_sem=ss.at[send_index],
            recv_sem=rs.at[recv_index],
            device_id=device,
            device_id_type=MESH,
        )

        @pl.when(here)
        def _():
            pltpu.make_async_copy(source, target, rs.at[recv_index]).start()

        @pl.when(jnp.logical_not(here))
        def _():
            copy.start()

        sent.append((here, copy))

    def arrived(source, target, index):
        pltpu.make_async_remote_copy(
            src_ref=source,
            dst_ref=target,
            send_sem=ss.at[index],
            recv_sem=rs.at[index],
            device_id=partner,
            device_id_type=MESH,
        ).wait_recv()

    def tokens_start(source, target):
        base = slot(4)
        core = lax.div(y, 2)
        block = lax.rem(y, 2)
        region = target.at[rows_at(block * 128, 128), own_lanes]
        for d in (1, 3, 2, 0):
            device = (x, core, z * 4 + mod4(y + d))
            index = base + block * 2 + r
            if d:
                copy = pltpu.make_async_remote_copy(
                    src_ref=source,
                    dst_ref=region,
                    send_sem=ss.at[base + d],
                    recv_sem=rs.at[index],
                    device_id=device,
                    device_id_type=MESH,
                )
                copy.start()
                sent.append((None, copy))
            else:
                place(source, region, device, base, index, core == r)
        return base

    def tokens_finish(source, target, base):
        for s in range(4):
            region = target.at[pl.ds((s // 2) * 128, 128), pl.ds((s % 2) * HALF, HALF)]
            arrived(source, region, base + s)

    def owners_start(source, target):
        base = slot(2)
        chip = 2 * r + lax.div(y, 2)
        region = target.at[rows_at(lax.rem(y, 2) * TO, TO)]
        for core in range(2):
            here = jnp.logical_and(chip == y, r == core)
            place(
                source.at[:, pl.ds(core * HALF, HALF)],
                region,
                (x, core, z * 4 + chip),
                base + core,
                base + lax.rem(y, 2),
                here,
            )
        return base

    def owners_finish(source, target, base):
        for s in range(2):
            arrived(source.at[:, pl.ds(0, HALF)], target.at[pl.ds(s * TO, TO)], base + s)

    local = [0]

    class Section:
        def __init__(self, source, region):
            self.source = source
            self.region = region

        def start(self):
            self.z = {d: push(self.source, self.region(z, r), z_peer(d)) for d in (1, 3, 2)}
            self.mine = pltpu.make_async_copy(self.source, self.region(z, r), ls.at[local[0]])
            local[0] += 1
            self.mine.start()
            self.cross = [push(self.source, self.region(z, r), partner)]

        def forward(self):
            for d in (1, 3, 2):
                self.z[d].wait_recv()
                region = self.region(mod4(z - d), r)
                self.cross.append(push(region, region, partner))

        def finish(self):
            self.mine.wait()
            for copy in self.cross:
                copy.wait_recv()

    class Split:
        def __init__(self, source, region):
            self.source = source
            self.region = region

        def start(self):
            quarter = self.source.at[:, lanes_at(x * 128, 128)]
            self.z = {
                d: push(quarter, self.region(z, r * HALF + x * 128, 128), z_peer(d))
                for d in (1, 3, 2)
            }
            whole = self.region(z, r * HALF, HALF)
            self.mine = pltpu.make_async_copy(self.source, whole, ls.at[local[0]])
            local[0] += 1
            self.mine.start()
            self.cross = [push(self.source, whole, partner)]

        def forward(self):
            self.x = []
            for d in (1, 3, 2):
                self.z[d].wait_recv()
                region = self.region(mod4(z - d), r * HALF + x * 128, 128)
                self.x += [push(region, region, x_peer(e)) for e in (1, 3, 2)]

        def across(self):
            for copy in self.x:
                copy.wait_recv()
            for d in (1, 3, 2):
                region = self.region(mod4(z - d), r * HALF, HALF)
                self.cross.append(push(region, region, partner))

        def finish(self):
            self.mine.wait()
            for copy in self.cross:
                copy.wait_recv()

    def mix_section(s, source):
        return Section(
            source, lambda zz, rr: w_mix.at[s, rows_at(zz * CB, CB), lanes_at(rr * HALF, HALF)]
        )

    mix = [mix_section(s, source) for s, source in enumerate((b_in, c_in, v_in, out_in))]
    gate = Section(
        gate_in, lambda zz, rr: w_feed.at[rows_at(zz * FB, FB), lanes_at(rr * HALF, HALF)]
    )
    up = Split(
        up_in, lambda zz, at, size: w_feed.at[rows_at(FQ + zz * FB, FB), lanes_at(at, size)]
    )
    down = Split(
        down_in,
        lambda zz, at, size: w_feed.at[rows_at(2 * FQ + zz * FB, FB), lanes_at(at, size)],
    )

    def scatter_start(k):
        return [
            push(halves.at[k, rows_at(mod4(y + d) * TO, TO)], recvs.at[k, d - 1], y_peer(d))
            for d in (1, 3, 2)
        ]

    def scatter_finish(k, copies):
        for copy in copies:
            copy.wait_recv()
        total = fulls[k, own_rows, :]
        for d in range(3):
            total = total + recvs[k, d].astype(F32)
        return total

    def gather_start(buffer):
        return [push(buffer.at[own_rows], buffer.at[own_rows], y_peer(d)) for d in (1, 3, 2)]

    def wait(copies):
        for copy in copies:
            copy.wait_recv()

    def product(k, value):
        def body(n):
            lanes = lanes_at(n * 256, 256)
            part = value(lanes)
            fulls[k, :, lanes] = part
            halves[k, :, lanes] = part.astype(BF16)

        loop(4, body)

    small[0:1, :] = first_in[...]
    small[1:2, :] = second_in[...]
    small[2:5, 0:CH] = taps_own[...]
    x_base = tokens_start(x_in, xs)
    for section in mix:
        section.start()
    up.start()
    small_copies = [push(small, gains.at[:, own_lanes], partner)]
    small_copies += [push(small, taps_in.at[d - 1], z_peer(d)) for d in (1, 3, 2)]
    gains[:, own_lanes] = small[...]
    st[...] = jnp.zeros((8, D), F32)
    here = ids[2 : 2 + TC, :]
    for k, first in enumerate((1, 0, 3, 4)):
        masks[k] = (ids[first : first + TC, :] == here).astype(F32)

    tokens_finish(x_in, xs, x_base)
    wait(small_copies)
    cot_base = tokens_start(cot_in, cs)
    first_gain = gains[0:1, :]
    second_gain = gains[1:2, :]
    taps = small[2:5, 0:CH]
    for d in range(3):
        taps = taps + taps_in[d, 2:5, 0:CH]

    def norm_body(i):
        rows = rows_at(i * 32, 32)
        value = xs[rows, :].astype(F32)
        scale = lax.rsqrt(jnp.sum(value * value, axis=1, keepdims=True) / D + EPSILON)
        fn[rows, :] = (value * scale * first_gain).astype(BF16)

    loop(8, norm_body)

    for section in mix:
        section.forward()
    down.start()
    gate.start()
    up.forward()
    for section in mix:
        section.finish()

    def pre_body(s):
        pre[s] = nt(fn[...], w_mix[s])

    loop(3, pre_body)

    gat[8 : 8 + TC, :] = pre[0] * pre[2]
    halo = push(gat.at[pl.ds(TC, 8)], gat.at[pl.ds(0, 8)], successor)
    halo.wait_recv()
    m1 = masks[0, :, 0:1]
    m2 = masks[1, :, 0:1]
    cvd[...] = (
        taps[0:1] * gat[8 : 8 + TC, :]
        + taps[1:2] * (m1 * gat[7 : 7 + TC, :])
        + taps[2:3] * (m2 * gat[6 : 6 + TC, :])
    )
    mx[...] = (pre[1] * cvd[...]).astype(BF16)
    product(0, lambda lanes: nn(mx[...], w_mix[3, :, lanes]))
    first_scatter = scatter_start(0)
    down.forward()

    residual = xs[own_rows, :].astype(F32) + scatter_finish(0, first_scatter)
    res[...] = residual
    second_scale = lax.rsqrt(jnp.sum(residual * residual, axis=1, keepdims=True) / D + EPSILON)
    sn[own_rows, :] = (residual * second_scale * second_gain).astype(BF16)
    sn_copies = gather_start(sn)

    gate.forward()
    up.across()
    tokens_finish(cot_in, cs, cot_base)
    gate.finish()
    up.finish()
    wait(sn_copies)

    def gu_body(n):
        at = n * 256
        gu[:, lanes_at(at, 256)] = nt(sn[...], w_feed[rows_at(at, 256), :])

    loop(9, gu_body)

    down.across()

    def hidden_body(i):
        rows = rows_at(i * 32, 32)
        g = gu[rows, 0:FQ]
        hid[rows, :] = (g * jax.nn.sigmoid(g) * gu[rows, FQ : 2 * FQ]).astype(BF16)

    loop(8, hidden_body)
    down.finish()

    def hg_body(n):
        at = n * 384
        gu[:, lanes_at(2 * FQ + at, 384)] = nt(cs[...], w_feed[rows_at(2 * FQ + at, 384), :])

    loop(3, hg_body)

    def delta_body(i):
        rows = rows_at(i * 32, 32)
        g = gu[rows, 0:FQ]
        u = gu[rows, FQ : 2 * FQ]
        hg = gu[rows, 2 * FQ : 3 * FQ]
        s = jax.nn.sigmoid(g)
        dg[rows, 0:FQ] = (hg * u * s * (1.0 + g * (1.0 - s))).astype(BF16)
        dg[rows, FQ : 2 * FQ] = (hg * (g * s)).astype(BF16)

    loop(8, delta_body)
    product(2, lambda lanes: nn(dg[...], w_feed[0 : 2 * FQ, lanes]))
    grad_scatter = scatter_start(2)
    product(1, lambda lanes: nn(hid[...], w_feed[2 * FQ : 3 * FQ, lanes]))
    block_scatter = scatter_start(1)

    def go_gu_body(n):
        at = n * 384
        go_f[rows_at(at, 384), :] = tn(dg[:, lanes_at(at, 384)], sn[:, other_lanes]).astype(BF16)

    def go_d_body(n):
        at = n * 384
        go_f[rows_at(2 * FQ + at, 384), :] = tn(
            hid[:, lanes_at(at, 384)], cs[:, other_lanes]
        ).astype(BF16)

    loop(6, go_gu_body)
    cross_gu = push(go_f.at[pl.ds(0, 2 * FQ)], cr_f.at[pl.ds(0, 2 * FQ)], partner)
    loop(3, go_d_body)
    cross_d = push(go_f.at[pl.ds(2 * FQ, FQ)], cr_f.at[pl.ds(2 * FQ, FQ)], partner)

    cross_gu.wait_recv()

    def s_gu_body(n):
        at = n * 384
        rows = rows_at(at, 384)
        s_f[rows, :] = (
            tn(dg[:, lanes_at(at, 384)], sn[:, own_lanes]) + cr_f[rows, :].astype(F32)
        ).astype(BF16)

    loop(6, s_gu_body)

    def feed_send(part):
        return [
            push(
                s_f.at[rows_at(part * FQ + mod4(z + d) * FB, FB)],
                zr_f.at[d - 1, pl.ds(part * FB, FB)],
                z_peer(d),
            )
            for d in (1, 3, 2)
        ]

    feed_z = feed_send(0) + feed_send(1)
    second_grad = scatter_finish(2, grad_scatter)
    residual = res[...]
    second_scale = lax.rsqrt(jnp.sum(residual * residual, axis=1, keepdims=True) / D + EPSILON)
    st[1:2, :] = jnp.sum(second_grad * residual * second_scale, axis=0, keepdims=True)
    weighted = second_grad * second_gain
    cube = second_scale * second_scale * second_scale
    residual_grad = (
        cs[own_rows, :].astype(F32)
        + second_scale * weighted
        - residual * cube * (jnp.sum(weighted * residual, axis=1, keepdims=True) / D)
    )
    rg[...] = residual_grad
    rh[own_rows, :] = residual_grad.astype(BF16)
    rh_copies = gather_start(rh)

    cross_d.wait_recv()

    def s_d_body(n):
        at = n * 384
        rows = rows_at(2 * FQ + at, 384)
        s_f[rows, :] = (
            tn(hid[:, lanes_at(at, 384)], cs[:, own_lanes]) + cr_f[rows, :].astype(F32)
        ).astype(BF16)

    loop(3, s_d_body)
    down_x = [
        push(s_f.at[pl.ds(2 * FQ, FQ), lanes_at(mod4(x + d) * 128, 128)], x1_d.at[d - 1], x_peer(d))
        for d in (1, 3, 2)
    ]

    wait(rh_copies)
    mixed_grad = nt(rh[...], w_mix[3])
    cg[0:TC, :] = mixed_grad * pre[1]
    halo_back = push(cg.at[pl.ds(0, 8)], cg.at[pl.ds(TC, 8)], predecessor)
    dm[1] = (mixed_grad * cvd[...]).astype(BF16)

    go_m[3] = tn(mx[...], rh[:, other_lanes]).astype(BF16)

    conv_grad = cg[0:TC, :]
    tap_lanes = lanes_at(y * CH, CH)
    st[2:3, tap_lanes] = jnp.sum(conv_grad * gat[8 : 8 + TC, :], axis=0, keepdims=True)
    st[3:4, tap_lanes] = jnp.sum(conv_grad * m1 * gat[7 : 7 + TC, :], axis=0, keepdims=True)
    st[4:5, tap_lanes] = jnp.sum(conv_grad * m2 * gat[6 : 6 + TC, :], axis=0, keepdims=True)
    halo_back.wait_recv()
    gated_grad = (
        taps[0:1] * conv_grad
        + taps[1:2] * (masks[2, :, 0:1] * cg[1 : 1 + TC, :])
        + taps[2:3] * (masks[3, :, 0:1] * cg[2 : 2 + TC, :])
    )
    dm[0] = (gated_grad * pre[2]).astype(BF16)
    dm[2] = (gated_grad * pre[0]).astype(BF16)

    def first_part(lanes):
        part = nn(dm[0], w_mix[0, :, lanes])
        part = part + nn(dm[1], w_mix[1, :, lanes])
        return part + nn(dm[2], w_mix[2, :, lanes])

    product(3, first_part)
    first_scatter = scatter_start(3)

    def go_m_body(s):
        go_m[s] = tn(dm[s], fn[:, other_lanes]).astype(BF16)

    loop(3, go_m_body)
    cross_m = push(go_m, cr_m, partner)

    x_lanes = lanes_at(x * 128, 128)
    wait(down_x)
    mine = s_f[2 * FQ : 3 * FQ, x_lanes].astype(F32)
    for d in range(3):
        mine = mine + x1_d[d].astype(F32)
    t_d[...] = mine.astype(BF16)
    down_z = [
        push(t_d.at[rows_at(mod4(z + d) * FB, FB)], z2_d.at[d - 1], z_peer(d)) for d in (1, 3, 2)
    ]

    cross_m.wait_recv()

    def s_m_body(s):
        s_m[s] = (tn(dm[s], fn[:, own_lanes]) + cr_m[s].astype(F32)).astype(BF16)

    loop(3, s_m_body)
    s_m[3] = (tn(mx[...], rh[:, own_lanes]) + cr_m[3].astype(F32)).astype(BF16)
    mix_z = [
        push(s_m.at[0:2, rows_at(mod4(z + d) * CB, CB), :], zr_m.at[d - 1], z_peer(d))
        for d in (1, 3, 2)
    ]
    mix_x = [
        push(s_m.at[2:4, :, lanes_at(mod4(x + d) * 128, 128)], x1_m.at[d - 1], x_peer(d))
        for d in (1, 3, 2)
    ]

    wait(feed_z)
    for part in range(2):
        mine = s_f[rows_at(part * FQ + z * FB, FB), :].astype(F32)
        at = part * FB
        for d in range(3):
            mine = mine + zr_f[d, at : at + FB, :].astype(F32)
        xs_f[at : at + FB, :] = mine.astype(BF16)
    feed_x = [
        push(xs_f.at[:, lanes_at(mod4(x + d) * 128, 128)], xr_f.at[d - 1], x_peer(d))
        for d in (1, 3, 2)
    ]

    bo_own[...] = (res[...] + scatter_finish(1, block_scatter)).astype(BF16)
    bo_base = owners_start(bo_own, block_o)

    first_grad = scatter_finish(3, first_scatter)
    value = xs[own_rows, :].astype(F32)
    first_scale = lax.rsqrt(jnp.sum(value * value, axis=1, keepdims=True) / D + EPSILON)
    st[0:1, :] = jnp.sum(first_grad * value * first_scale, axis=0, keepdims=True)
    weighted = first_grad * first_gain
    cube = first_scale * first_scale * first_scale
    ig_own[...] = (
        rg[...]
        + first_scale * weighted
        - value * cube * (jnp.sum(weighted * value, axis=1, keepdims=True) / D)
    )
    ig_base = owners_start(ig_own, input_o)
    stat_copies = [push(st, st_y.at[0], partner)]
    for d in (1, 2, 3):
        stat_copies.append(push(st, st_y.at[2 * d - 1], y_peer(d)))
        stat_copies.append(push(st, st_y.at[2 * d], (x, other, z * 4 + mod4(y + d))))

    wait(mix_x)
    mine = s_m[2:4, :, x_lanes].astype(F32)
    for d in range(3):
        mine = mine + x1_m[d].astype(F32)
    t_m[...] = mine.astype(BF16)
    mix_zz = [
        push(t_m.at[:, rows_at(mod4(z + d) * CB, CB), :], z2_m.at[d - 1], z_peer(d))
        for d in (1, 3, 2)
    ]
    wait(mix_z)
    mine = s_m[0:2, rows_at(z * CB, CB), :].astype(F32)
    for d in range(3):
        mine = mine + zr_m[d].astype(F32)
    xs_m[...] = mine.astype(BF16)
    mix_xx = [
        push(xs_m.at[:, :, lanes_at(mod4(x + d) * 128, 128)], xr_m.at[d - 1], x_peer(d))
        for d in (1, 3, 2)
    ]

    wait(feed_x)
    mine = xs_f[:, x_lanes].astype(F32)
    for d in range(3):
        mine = mine + xr_f[d].astype(F32)
    xf_f[0 : 2 * FB, x_lanes] = mine.astype(BF16)
    wait(down_z)
    mine = t_d[rows_at(z * FB, FB), :].astype(F32)
    for d in range(3):
        mine = mine + z2_d[d].astype(F32)
    xf_f[2 * FB : 3 * FB, x_lanes] = mine.astype(BF16)
    feed_g = [push(xf_f.at[:, x_lanes], xf_f.at[:, x_lanes], x_peer(d)) for d in (1, 3, 2)]

    wait(stat_copies)
    total = st[...]
    for i in range(7):
        total = total + st_y[i]
    st_z[3] = total
    stat_copies = [push(st_z.at[3], st_z.at[d - 1], z_peer(d)) for d in (1, 3, 2)]

    wait(mix_zz)
    mine = t_m[:, rows_at(z * CB, CB), :].astype(F32)
    for d in range(3):
        mine = mine + z2_m[d].astype(F32)
    xf_m[2:4, :, x_lanes] = mine.astype(BF16)
    wait(mix_xx)
    mine = xs_m[:, :, x_lanes].astype(F32)
    for d in range(3):
        mine = mine + xr_m[d].astype(F32)
    xf_m[0:2, :, x_lanes] = mine.astype(BF16)
    mix_g = [push(xf_m.at[:, :, x_lanes], xf_m.at[:, :, x_lanes], x_peer(d)) for d in (1, 3, 2)]

    wait(stat_copies)
    st_x[3] = st_z[0] + st_z[1] + st_z[2] + st_z[3]
    stat_copies = [push(st_x.at[3], st_x.at[d - 1], x_peer(d)) for d in (1, 3, 2)]

    owners_finish(bo_own, block_o, bo_base)
    owners_finish(ig_own, input_o, ig_base)
    wait(feed_g)
    for part, target in enumerate((gate_o, up_o, down_o)):
        target[...] = xf_f[part * FB : (part + 1) * FB, :].astype(F32)
    wait(mix_g)
    for part, target in enumerate((b_o, c_o, v_o, out_o)):
        target[...] = xf_m[part].astype(F32)
    wait(stat_copies)
    stats_o[...] = st_x[0] + st_x[1] + st_x[2] + st_x[3]

    for here, copy in sent:
        if here is None:
            copy.wait_send()
        else:

            @pl.when(jnp.logical_not(here))
            def _(copy=copy):
                copy.wait_send()


def shards(
    hidden_in,
    segment_ids,
    first_gain,
    mixer_b,
    mixer_c,
    mixer_v,
    conv_kernel,
    mixer_out,
    second_gain,
    gate_weight,
    up_weight,
    down_weight,
    cotangent,
):
    r = lax.axis_index("row")
    col = lax.axis_index("col")
    z = col // 4
    y = col % 4
    ids = jnp.pad(segment_ids[0], ((2, 6),), constant_values=-1)
    ids = lax.dynamic_slice_in_dim(ids, z * 512 + r * TC, TC + 8, 0)
    ids = jnp.broadcast_to(ids[:, None], (TC + 8, 128))
    at_z = lax.broadcasted_iota(jnp.int32, (3, CH), 1) // CB == z
    taps = jnp.where(at_z, jnp.tile(conv_kernel, (1, CH // CB)), 0.0)
    vmem = pl.BlockSpec(memory_space=pltpu.VMEM)
    shape = jax.ShapeDtypeStruct
    scratch = [
        ((8, HALF), F32),
        ((4, TC, 128), F32),
        ((TC, D), BF16),
        ((TC, D), BF16),
        ((8, D), F32),
        ((3, 8, HALF), F32),
        ((4, CH, D), BF16),
        ((3 * FQ, D), BF16),
        ((TC, D), BF16),
        ((3, TC, CH), F32),
        ((TC + 8, CH), F32),
        ((TC, CH), F32),
        ((TC, CH), BF16),
        ((TO, D), F32),
        ((TC, D), BF16),
        ((TC, 3 * FQ), F32),
        ((TC, FQ), BF16),
        ((TC, 2 * FQ), BF16),
        ((4, TC, D), F32),
        ((4, TC, D), BF16),
        ((4, 3, TO, D), BF16),
        ((TO, D), F32),
        ((TC, D), BF16),
        ((TC + 8, CH), F32),
        ((3, TC, CH), BF16),
        ((3 * FQ, HALF), BF16),
        ((3 * FQ, HALF), BF16),
        ((3 * FQ, HALF), BF16),
        ((3, 2 * FB, HALF), BF16),
        ((2 * FB, HALF), BF16),
        ((3, 2 * FB, 128), BF16),
        ((3 * FB, HALF), BF16),
        ((3, FQ, 128), BF16),
        ((FQ, 128), BF16),
        ((3, FB, 128), BF16),
        ((4, CH, HALF), BF16),
        ((4, CH, HALF), BF16),
        ((4, CH, HALF), BF16),
        ((3, 2, CB, HALF), BF16),
        ((2, CB, HALF), BF16),
        ((3, 2, CB, 128), BF16),
        ((4, CB, HALF), BF16),
        ((3, 2, CH, 128), BF16),
        ((2, CH, 128), BF16),
        ((3, 2, CB, 128), BF16),
        ((8, D), F32),
        ((7, 8, D), F32),
        ((4, 8, D), F32),
        ((4, 8, D), F32),
        ((TO, D), BF16),
        ((TO, D), F32),
    ]
    block_out, input_grad, b_g, c_g, v_g, out_g, gate_g, up_g, down_g, stats = pl.pallas_call(
        kernel,
        out_shape=(
            shape((128, HALF), BF16),
            shape((128, HALF), F32),
            *[shape((CB, HALF), F32)] * 4,
            *[shape((FB, HALF), F32)] * 3,
            shape((8, D), F32),
        ),
        in_specs=[vmem] * 13,
        out_specs=(vmem,) * 10,
        scratch_shapes=[pltpu.VMEM(s, t) for s, t in scratch]
        + [
            pltpu.SemaphoreType.DMA((COPIES,)),
            pltpu.SemaphoreType.DMA((COPIES,)),
            pltpu.SemaphoreType.DMA((7,)),
        ],
        compiler_params=pltpu.CompilerParams(
            collective_id=0, has_side_effects=True, vmem_limit_bytes=62 * 2**20
        ),
    )(
        hidden_in,
        cotangent,
        ids,
        first_gain[None],
        second_gain[None],
        taps,
        mixer_b.T,
        mixer_c.T,
        mixer_v.T,
        mixer_out,
        gate_weight.T,
        up_weight.T,
        down_weight,
    )
    mine = lax.dynamic_slice_in_dim(stats[:2], r * HALF, HALF, 1)
    kernel_grad = lax.dynamic_slice(stats, (2, y * CH + z * CB + r * 32), (3, 32))
    return (
        block_out,
        input_grad,
        mine[0],
        b_g.T,
        c_g.T,
        v_g.T,
        kernel_grad,
        out_g,
        mine[1],
        gate_g.T,
        up_g.T,
        down_g,
    )


def solution(mesh):
    return jax.shard_map(
        shards,
        mesh=mesh,
        in_specs=(
            P(("dp", "col"), "row"),
            P("dp", None),
            P("row"),
            P("row", "col"),
            P("row", "col"),
            P("row", "col"),
            P(None, "col"),
            P("col", "row"),
            P("row"),
            P("row", "col"),
            P("row", "col"),
            P("col", "row"),
            P(("dp", "col"), "row"),
        ),
        out_specs=(
            P(("dp", "col"), "row"),
            P(("dp", "col"), "row"),
            P("row"),
            P("row", "col"),
            P("row", "col"),
            P("row", "col"),
            P(None, ("col", "row")),
            P("col", "row"),
            P("row"),
            P("row", "col"),
            P("row", "col"),
            P("col", "row"),
        ),
        check_vma=False,
    )
```

```python
import jax
import jax.numpy as jnp
from jax import lax
from jax.experimental import pallas as pl
from jax.experimental.pallas import tpu as pltpu
from jax.sharding import PartitionSpec as P

EPSILON = 1e-05
MESH = pl.DeviceIdType.MESH
F32 = jnp.float32
BF16 = jnp.bfloat16

D = 1024
HALF = 512
CH = 256
CB = 64
FQ = 1152
FB = 288
TC = 256
TO = 64
COPIES = 256


def mod4(value):
    return lax.rem(value + 4, 4)


def nt(a, b):
    return lax.dot_general(a, b, (((1,), (1,)), ((), ())), preferred_element_type=F32)


def nn(a, b):
    return lax.dot_general(a, b, (((1,), (0,)), ((), ())), preferred_element_type=F32)


def tn(a, b):
    return lax.dot_general(a, b, (((0,), (0,)), ((), ())), preferred_element_type=F32)


def loop(count, body):
    def step(i, carry):
        body(i)
        return carry

    lax.fori_loop(0, count, step, 0)


def rows_at(start, size, multiple=32):
    return pl.ds(pl.multiple_of(start, multiple), size)


def lanes_at(start, size):
    return pl.ds(pl.multiple_of(start, 128), size)


def kernel(
    x_in,
    cot_in,
    ids,
    first_in,
    second_in,
    taps_own,
    b_in,
    c_in,
    v_in,
    out_in,
    gate_in,
    up_in,
    down_in,
    block_o,
    input_o,
    mix_o,
    feed_o,
    stats_o,
    small,
    masks,
    xs,
    cs,
    gains,
    taps_in,
    w_mix,
    w_feed,
    fn,
    pre,
    gat,
    cvd,
    mx,
    res,
    sn,
    gu,
    hid,
    dg,
    fulls,
    halves,
    recvs,
    rg,
    rh,
    cg,
    dm,
    go_f,
    cr_f,
    s_f,
    zr_f,
    xs_f,
    xr_f,
    xf_f,
    x1_d,
    t_d,
    z2_d,
    go_m,
    cr_m,
    s_m,
    zr_m,
    xs_m,
    xr_m,
    xf_m,
    st,
    st_y,
    st_z,
    st_x,
    bo_own,
    ig_own,
    ss,
    rs,
    ls,
):
    x = lax.axis_index("dp")
    r = lax.axis_index("row")
    col = lax.axis_index("col")
    z = lax.div(col, 4)
    y = lax.rem(col, 4)
    other = 1 - r
    own_lanes = lanes_at(r * HALF, HALF)
    other_lanes = lanes_at(other * HALF, HALF)
    own_rows = rows_at(y * TO, TO)

    def y_peer(d):
        return (x, r, z * 4 + mod4(y + d))

    def z_peer(d):
        return (x, r, mod4(z + d) * 4 + y)

    def x_peer(d):
        return (mod4(x + d), r, col)

    partner = (x, other, col)
    successor = (x, other, mod4(z + r) * 4 + y)
    predecessor = (x, other, mod4(z + r + 3) * 4 + y)
    halo_extra = (x, other, mod4(z + 2 * r - 1) * 4 + y)

    barrier = pltpu.get_barrier_semaphore()
    greeted = [partner, halo_extra]
    for d in (1, 2, 3):
        greeted += [y_peer(d), (x, other, z * 4 + mod4(y + d)), z_peer(d), x_peer(d)]
    for device in greeted:
        pl.semaphore_signal(barrier, inc=1, device_id=device, device_id_type=MESH)
    pl.semaphore_wait(barrier, len(greeted))

    used = [0]
    sent = []

    def slot(count=1):
        first = used[0]
        used[0] += count
        return first

    def push(source, target, device, index=None):
        i = slot() if index is None else index
        copy = pltpu.make_async_remote_copy(
            src_ref=source,
            dst_ref=target,
            send_sem=ss.at[i],
            recv_sem=rs.at[i],
            device_id=device,
            device_id_type=MESH,
        )
        copy.start()
        sent.append((None, copy))
        return copy

    def place(source, target, device, send_index, recv_index, here):
        copy = pltpu.make_async_remote_copy(
            src_ref=source,
            dst_ref=target,
            send_sem=ss.at[send_index],
            recv_sem=rs.at[recv_index],
            device_id=device,
            device_id_type=MESH,
        )

        @pl.when(here)
        def _():
            pltpu.make_async_copy(source, target, rs.at[recv_index]).start()

        @pl.when(jnp.logical_not(here))
        def _():
            copy.start()

        sent.append((here, copy))

    def arrived(source, target, index):
        pltpu.make_async_remote_copy(
            src_ref=source,
            dst_ref=target,
            send_sem=ss.at[index],
            recv_sem=rs.at[index],
            device_id=partner,
            device_id_type=MESH,
        ).wait_recv()

    def tokens_start(source, target):
        base = slot(4)
        core = lax.div(y, 2)
        block = lax.rem(y, 2)
        region = target.at[rows_at(block * 128, 128), own_lanes]
        for d in (1, 3, 2, 0):
            device = (x, core, z * 4 + mod4(y + d))
            index = base + block * 2 + r
            if d:
                copy = pltpu.make_async_remote_copy(
                    src_ref=source,
                    dst_ref=region,
                    send_sem=ss.at[base + d],
                    recv_sem=rs.at[index],
                    device_id=device,
                    device_id_type=MESH,
                )
                copy.start()
                sent.append((None, copy))
            else:
                place(source, region, device, base, index, core == r)
        return base

    def tokens_finish(source, target, base):
        for s in range(4):
            region = target.at[pl.ds((s // 2) * 128, 128), pl.ds((s % 2) * HALF, HALF)]
            arrived(source, region, base + s)

    def owners_start(source, target):
        base = slot(2)
        chip = 2 * r + lax.div(y, 2)
        region = target.at[rows_at(lax.rem(y, 2) * TO, TO)]
        for core in range(2):
            here = jnp.logical_and(chip == y, r == core)
            place(
                source.at[:, pl.ds(core * HALF, HALF)],
                region,
                (x, core, z * 4 + chip),
                base + core,
                base + lax.rem(y, 2),
                here,
            )
        return base

    def owners_finish(source, target, base):
        for s in range(2):
            arrived(source.at[:, pl.ds(0, HALF)], target.at[pl.ds(s * TO, TO)], base + s)

    local = [0]

    class Section:
        def __init__(self, source, region):
            self.source = source
            self.region = region

        def start(self):
            self.z = {d: push(self.source, self.region(z, r), z_peer(d)) for d in (1, 3, 2)}
            self.mine = pltpu.make_async_copy(self.source, self.region(z, r), ls.at[local[0]])
            local[0] += 1
            self.mine.start()
            self.cross = [push(self.source, self.region(z, r), partner)]

        def forward(self):
            for d in (1, 3, 2):
                self.z[d].wait_recv()
                region = self.region(mod4(z - d), r)
                self.cross.append(push(region, region, partner))

        def finish(self):
            self.mine.wait()
            for copy in self.cross:
                copy.wait_recv()

    class Split:
        def __init__(self, source, region):
            self.source = source
            self.region = region

        def start(self):
            quarter = self.source.at[:, lanes_at(x * 128, 128)]
            self.z = {
                d: push(quarter, self.region(z, r * HALF + x * 128, 128), z_peer(d))
                for d in (1, 3, 2)
            }
            whole = self.region(z, r * HALF, HALF)
            self.mine = pltpu.make_async_copy(self.source, whole, ls.at[local[0]])
            local[0] += 1
            self.mine.start()
            self.cross = [push(self.source, whole, partner)]

        def forward(self):
            self.x = []
            for d in (1, 3, 2):
                self.z[d].wait_recv()
                region = self.region(mod4(z - d), r * HALF + x * 128, 128)
                self.x += [push(region, region, x_peer(e)) for e in (1, 3, 2)]

        def across(self):
            for copy in self.x:
                copy.wait_recv()
            for d in (1, 3, 2):
                region = self.region(mod4(z - d), r * HALF, HALF)
                self.cross.append(push(region, region, partner))

        def finish(self):
            self.mine.wait()
            for copy in self.cross:
                copy.wait_recv()

    def mix_section(s, source):
        return Section(
            source, lambda zz, rr: w_mix.at[s, rows_at(zz * CB, CB), lanes_at(rr * HALF, HALF)]
        )

    mix = [mix_section(s, source) for s, source in enumerate((b_in, c_in, v_in, out_in))]
    gate = Section(
        gate_in, lambda zz, rr: w_feed.at[rows_at(zz * FB, FB), lanes_at(rr * HALF, HALF)]
    )
    up = Split(
        up_in, lambda zz, at, size: w_feed.at[rows_at(FQ + zz * FB, FB), lanes_at(at, size)]
    )
    down = Split(
        down_in,
        lambda zz, at, size: w_feed.at[rows_at(2 * FQ + zz * FB, FB), lanes_at(at, size)],
    )

    def scatter_start(k):
        return [
            push(halves.at[k, rows_at(mod4(y + d) * TO, TO)], recvs.at[k, d - 1], y_peer(d))
            for d in (1, 3, 2)
        ]

    def scatter_finish(k, copies):
        for copy in copies:
            copy.wait_recv()
        total = fulls[k, own_rows, :]
        for d in range(3):
            total = total + recvs[k, d].astype(F32)
        return total

    def gather_start(buffer):
        return [push(buffer.at[own_rows], buffer.at[own_rows], y_peer(d)) for d in (1, 3, 2)]

    def wait(copies):
        for copy in copies:
            copy.wait_recv()

    def product(k, value):
        def body(n):
            lanes = lanes_at(n * 256, 256)
            part = value(lanes)
            fulls[k, :, lanes] = part
            halves[k, :, lanes] = part.astype(BF16)

        loop(4, body)

    small[0:1, :] = first_in[...]
    small[1:2, :] = second_in[...]
    small[2:5, 0:CH] = taps_own[...]
    x_base = tokens_start(x_in, xs)
    for section in mix:
        section.start()
    up.start()
    small_copies = [push(small, gains.at[:, own_lanes], partner)]
    small_copies += [push(small, taps_in.at[d - 1], z_peer(d)) for d in (1, 3, 2)]
    gains[:, own_lanes] = small[...]
    st[...] = jnp.zeros((8, D), F32)
    here = ids[2 : 2 + TC, :]
    for k, first in enumerate((1, 0, 3, 4)):
        masks[k] = (ids[first : first + TC, :] == here).astype(F32)

    tokens_finish(x_in, xs, x_base)
    wait(small_copies)
    cot_base = tokens_start(cot_in, cs)
    first_gain = gains[0:1, :]
    second_gain = gains[1:2, :]
    taps = small[2:5, 0:CH]
    for d in range(3):
        taps = taps + taps_in[d, 2:5, 0:CH]

    def norm_body(i):
        rows = rows_at(i * 32, 32)
        value = xs[rows, :].astype(F32)
        scale = lax.rsqrt(jnp.sum(value * value, axis=1, keepdims=True) / D + EPSILON)
        fn[rows, :] = (value * scale * first_gain).astype(BF16)

    loop(8, norm_body)

    for section in mix:
        section.forward()
    down.start()
    gate.start()
    up.forward()
    for section in mix:
        section.finish()

    def pre_body(s):
        pre[s] = nt(fn[...], w_mix[s])

    loop(3, pre_body)

    gat[8 : 8 + TC, :] = pre[0] * pre[2]
    halo = push(gat.at[pl.ds(TC, 8)], gat.at[pl.ds(0, 8)], successor)
    halo.wait_recv()
    m1 = masks[0, :, 0:1]
    m2 = masks[1, :, 0:1]
    cvd[...] = (
        taps[0:1] * gat[8 : 8 + TC, :]
        + taps[1:2] * (m1 * gat[7 : 7 + TC, :])
        + taps[2:3] * (m2 * gat[6 : 6 + TC, :])
    )
    mx[...] = (pre[1] * cvd[...]).astype(BF16)
    product(0, lambda lanes: nn(mx[...], w_mix[3, :, lanes]))
    first_scatter = scatter_start(0)
    down.forward()

    residual = xs[own_rows, :].astype(F32) + scatter_finish(0, first_scatter)
    res[...] = residual
    second_scale = lax.rsqrt(jnp.sum(residual * residual, axis=1, keepdims=True) / D + EPSILON)
    sn[own_rows, :] = (residual * second_scale * second_gain).astype(BF16)
    sn_copies = gather_start(sn)

    gate.forward()
    up.across()
    tokens_finish(cot_in, cs, cot_base)
    gate.finish()
    up.finish()
    wait(sn_copies)

    def gu_body(n):
        at = n * 256
        gu[:, lanes_at(at, 256)] = nt(sn[...], w_feed[rows_at(at, 256), :])

    loop(9, gu_body)

    down.across()

    def hidden_body(i):
        rows = rows_at(i * 32, 32)
        g = gu[rows, 0:FQ]
        hid[rows, :] = (g * jax.nn.sigmoid(g) * gu[rows, FQ : 2 * FQ]).astype(BF16)

    loop(8, hidden_body)
    down.finish()

    def hg_body(n):
        at = n * 384
        gu[:, lanes_at(2 * FQ + at, 384)] = nt(cs[...], w_feed[rows_at(2 * FQ + at, 384), :])

    loop(3, hg_body)

    def delta_body(i):
        rows = rows_at(i * 32, 32)
        g = gu[rows, 0:FQ]
        u = gu[rows, FQ : 2 * FQ]
        hg = gu[rows, 2 * FQ : 3 * FQ]
        s = jax.nn.sigmoid(g)
        dg[rows, 0:FQ] = (hg * u * s * (1.0 + g * (1.0 - s))).astype(BF16)
        dg[rows, FQ : 2 * FQ] = (hg * (g * s)).astype(BF16)

    loop(8, delta_body)
    product(2, lambda lanes: nn(dg[...], w_feed[0 : 2 * FQ, lanes]))
    grad_scatter = scatter_start(2)
    def go_gu_body(n):
        at = n * 384
        go_f[rows_at(at, 384), :] = tn(dg[:, lanes_at(at, 384)], sn[:, other_lanes]).astype(BF16)

    def go_d_body(n):
        at = n * 384
        go_f[rows_at(2 * FQ + at, 384), :] = tn(
            hid[:, lanes_at(at, 384)], cs[:, other_lanes]
        ).astype(BF16)

    loop(6, go_gu_body)
    cross_gu = push(go_f.at[pl.ds(0, 2 * FQ)], cr_f.at[pl.ds(0, 2 * FQ)], partner)
    loop(3, go_d_body)
    cross_d = push(go_f.at[pl.ds(2 * FQ, FQ)], cr_f.at[pl.ds(2 * FQ, FQ)], partner)

    cross_gu.wait_recv()

    def s_gu_body(n):
        at = n * 384
        rows = rows_at(at, 384)
        s_f[rows, :] = (
            tn(dg[:, lanes_at(at, 384)], sn[:, own_lanes]) + cr_f[rows, :].astype(F32)
        ).astype(BF16)

    loop(6, s_gu_body)

    def feed_send(part):
        return [
            push(
                s_f.at[rows_at(part * FQ + mod4(z + d) * FB, FB)],
                zr_f.at[d - 1, pl.ds(part * FB, FB)],
                z_peer(d),
            )
            for d in (1, 3, 2)
        ]

    feed_z = feed_send(0) + feed_send(1)
    second_grad = scatter_finish(2, grad_scatter)
    residual = res[...]
    second_scale = lax.rsqrt(jnp.sum(residual * residual, axis=1, keepdims=True) / D + EPSILON)
    st[1:2, :] = jnp.sum(second_grad * residual * second_scale, axis=0, keepdims=True)
    weighted = second_grad * second_gain
    cube = second_scale * second_scale * second_scale
    residual_grad = (
        cs[own_rows, :].astype(F32)
        + second_scale * weighted
        - residual * cube * (jnp.sum(weighted * residual, axis=1, keepdims=True) / D)
    )
    rg[...] = residual_grad
    rh[own_rows, :] = residual_grad.astype(BF16)
    rh_copies = gather_start(rh)

    cross_d.wait_recv()

    def s_d_body(n):
        at = n * 384
        rows = rows_at(2 * FQ + at, 384)
        s_f[rows, :] = (
            tn(hid[:, lanes_at(at, 384)], cs[:, own_lanes]) + cr_f[rows, :].astype(F32)
        ).astype(BF16)

    loop(3, s_d_body)
    down_x = [
        push(s_f.at[pl.ds(2 * FQ, FQ), lanes_at(mod4(x + d) * 128, 128)], x1_d.at[d - 1], x_peer(d))
        for d in (1, 3, 2)
    ]
    product(1, lambda lanes: nn(hid[...], w_feed[2 * FQ : 3 * FQ, lanes]))
    block_scatter = scatter_start(1)

    wait(rh_copies)
    mixed_grad = nt(rh[...], w_mix[3])
    cg[0:TC, :] = mixed_grad * pre[1]
    halo_back = push(cg.at[pl.ds(0, 8)], cg.at[pl.ds(TC, 8)], predecessor)
    dm[1] = (mixed_grad * cvd[...]).astype(BF16)

    go_m[3] = tn(mx[...], rh[:, other_lanes]).astype(BF16)

    conv_grad = cg[0:TC, :]
    tap_lanes = lanes_at(y * CH, CH)
    st[2:3, tap_lanes] = jnp.sum(conv_grad * gat[8 : 8 + TC, :], axis=0, keepdims=True)
    st[3:4, tap_lanes] = jnp.sum(conv_grad * m1 * gat[7 : 7 + TC, :], axis=0, keepdims=True)
    st[4:5, tap_lanes] = jnp.sum(conv_grad * m2 * gat[6 : 6 + TC, :], axis=0, keepdims=True)
    halo_back.wait_recv()
    gated_grad = (
        taps[0:1] * conv_grad
        + taps[1:2] * (masks[2, :, 0:1] * cg[1 : 1 + TC, :])
        + taps[2:3] * (masks[3, :, 0:1] * cg[2 : 2 + TC, :])
    )
    dm[0] = (gated_grad * pre[2]).astype(BF16)
    dm[2] = (gated_grad * pre[0]).astype(BF16)

    def first_part(lanes):
        part = nn(dm[0], w_mix[0, :, lanes])
        part = part + nn(dm[1], w_mix[1, :, lanes])
        return part + nn(dm[2], w_mix[2, :, lanes])

    product(3, first_part)
    first_scatter = scatter_start(3)

    def go_m_body(s):
        go_m[s] = tn(dm[s], fn[:, other_lanes]).astype(BF16)

    loop(3, go_m_body)
    cross_m = push(go_m, cr_m, partner)

    x_lanes = lanes_at(x * 128, 128)
    wait(down_x)
    mine = s_f[2 * FQ : 3 * FQ, x_lanes].astype(F32)
    for d in range(3):
        mine = mine + x1_d[d].astype(F32)
    t_d[...] = mine.astype(BF16)
    down_z = [
        push(t_d.at[rows_at(mod4(z + d) * FB, FB)], z2_d.at[d - 1], z_peer(d)) for d in (1, 3, 2)
    ]

    wait(feed_z)
    for part in range(2):
        mine = s_f[rows_at(part * FQ + z * FB, FB), :].astype(F32)
        at = part * FB
        for d in range(3):
            mine = mine + zr_f[d, at : at + FB, :].astype(F32)
        xs_f[at : at + FB, :] = mine.astype(BF16)
    feed_x = [
        push(xs_f.at[:, lanes_at(mod4(x + d) * 128, 128)], xr_f.at[d - 1], x_peer(d))
        for d in (1, 3, 2)
    ]

    cross_m.wait_recv()

    def s_m_body(s):
        s_m[s] = (tn(dm[s], fn[:, own_lanes]) + cr_m[s].astype(F32)).astype(BF16)

    loop(3, s_m_body)
    s_m[3] = (tn(mx[...], rh[:, own_lanes]) + cr_m[3].astype(F32)).astype(BF16)
    mix_z = [
        push(s_m.at[:, rows_at(mod4(z + d) * CB, CB), :], zr_m.at[d - 1], z_peer(d))
        for d in (1, 3, 2)
    ]

    kept = []

    def spread(source, target):
        copy = pltpu.make_async_copy(source, target, ls.at[local[0]])
        local[0] += 1
        copy.start()
        kept.append(copy)
        return [push(source, target, x_peer(d)) for d in (1, 3, 2)]

    wait(down_z)
    mine = t_d[rows_at(z * FB, FB), :].astype(F32)
    for d in range(3):
        mine = mine + z2_d[d].astype(F32)
    xf_f[2 * FB : 3 * FB, :] = mine.astype(BF16)
    down_rows = pl.ds(2 * FB, FB)
    feed_g = spread(xf_f.at[down_rows], feed_o.at[down_rows, x_lanes])

    bo_own[...] = (res[...] + scatter_finish(1, block_scatter)).astype(BF16)
    bo_base = owners_start(bo_own, block_o)

    first_grad = scatter_finish(3, first_scatter)
    value = xs[own_rows, :].astype(F32)
    first_scale = lax.rsqrt(jnp.sum(value * value, axis=1, keepdims=True) / D + EPSILON)
    st[0:1, :] = jnp.sum(first_grad * value * first_scale, axis=0, keepdims=True)
    weighted = first_grad * first_gain
    cube = first_scale * first_scale * first_scale
    ig_own[...] = (
        rg[...]
        + first_scale * weighted
        - value * cube * (jnp.sum(weighted * value, axis=1, keepdims=True) / D)
    )
    ig_base = owners_start(ig_own, input_o)
    stat_copies = [push(st, st_y.at[0], partner)]
    for d in (1, 2, 3):
        stat_copies.append(push(st, st_y.at[2 * d - 1], y_peer(d)))
        stat_copies.append(push(st, st_y.at[2 * d], (x, other, z * 4 + mod4(y + d))))

    wait(feed_x)
    mine = xs_f[:, x_lanes].astype(F32)
    for d in range(3):
        mine = mine + xr_f[d].astype(F32)
    xf_f[0 : 2 * FB, :] = mine.astype(BF16)
    gate_rows = pl.ds(0, 2 * FB)
    feed_g += spread(xf_f.at[gate_rows], feed_o.at[gate_rows, x_lanes])

    wait(stat_copies)
    total = st[...]
    for i in range(7):
        total = total + st_y[i]
    st_z[3] = total
    stat_copies = [push(st_z.at[3], st_z.at[d - 1], z_peer(d)) for d in (1, 3, 2)]

    wait(mix_z)
    mine = s_m[:, rows_at(z * CB, CB), :].astype(F32)
    for d in range(3):
        mine = mine + zr_m[d].astype(F32)
    xs_m[...] = mine.astype(BF16)
    mix_x = [
        push(xs_m.at[:, :, lanes_at(mod4(x + d) * 128, 128)], xr_m.at[d - 1], x_peer(d))
        for d in (1, 3, 2)
    ]
    wait(stat_copies)
    st_x[3] = st_z[0] + st_z[1] + st_z[2] + st_z[3]
    stat_copies = [push(st_x.at[3], st_x.at[d - 1], x_peer(d)) for d in (1, 3, 2)]

    wait(mix_x)
    mine = xs_m[:, :, x_lanes].astype(F32)
    for d in range(3):
        mine = mine + xr_m[d].astype(F32)
    xf_m[...] = mine.astype(BF16)
    mix_g = spread(xf_m, mix_o.at[:, :, x_lanes])

    wait(stat_copies)
    stats_o[...] = st_x[0] + st_x[1] + st_x[2] + st_x[3]
    owners_finish(bo_own, block_o, bo_base)
    owners_finish(ig_own, input_o, ig_base)
    wait(feed_g)
    wait(mix_g)
    for copy in kept:
        copy.wait()

    for here, copy in sent:
        if here is None:
            copy.wait_send()
        else:

            @pl.when(jnp.logical_not(here))
            def _(copy=copy):
                copy.wait_send()


def finish(
    block_i,
    input_i,
    mix_i,
    feed_i,
    stats,
    block_o,
    input_o,
    b_o,
    c_o,
    v_o,
    out_o,
    gate_o,
    up_o,
    down_o,
    first_o,
    second_o,
    taps_o,
):
    r = lax.axis_index("row")
    col = lax.axis_index("col")
    z = lax.div(col, 4)
    y = lax.rem(col, 4)
    block_o[...] = block_i[...]
    input_o[...] = input_i[...]
    lanes = lanes_at(r * HALF, HALF)
    first_o[...] = stats[0:1, lanes]
    second_o[...] = stats[1:2, lanes]
    window = stats[2:5, lanes_at(y * CH + lax.div(z, 2) * 128, 128)]
    place = lax.rem(z, 2) * 2 + r
    total = jnp.zeros((3, 32), F32)
    for k in range(4):
        total = total + jnp.where(place == k, window[:, k * 32 : (k + 1) * 32], 0.0)
    taps_o[...] = total
    for part, target in enumerate((gate_o, up_o, down_o)):
        target[...] = feed_i[part * FB : (part + 1) * FB, :].astype(F32)
    for part, target in enumerate((b_o, c_o, v_o, out_o)):
        target[...] = mix_i[part].astype(F32)


def shards(
    hidden_in,
    segment_ids,
    first_gain,
    mixer_b,
    mixer_c,
    mixer_v,
    conv_kernel,
    mixer_out,
    second_gain,
    gate_weight,
    up_weight,
    down_weight,
    cotangent,
):
    r = lax.axis_index("row")
    col = lax.axis_index("col")
    z = col // 4
    y = col % 4
    ids = jnp.pad(segment_ids[0], ((2, 6),), constant_values=-1)
    ids = lax.dynamic_slice_in_dim(ids, z * 512 + r * TC, TC + 8, 0)
    ids = jnp.broadcast_to(ids[:, None], (TC + 8, 128))
    at_z = lax.broadcasted_iota(jnp.int32, (3, CH), 1) // CB == z
    taps = jnp.where(at_z, jnp.tile(conv_kernel, (1, CH // CB)), 0.0)
    vmem = pl.BlockSpec(memory_space=pltpu.VMEM)
    whole = pl.BlockSpec(memory_space=pl.ANY)
    shape = jax.ShapeDtypeStruct
    scratch = [
        ((8, HALF), F32),
        ((4, TC, 128), F32),
        ((TC, D), BF16),
        ((TC, D), BF16),
        ((8, D), F32),
        ((3, 8, HALF), F32),
        ((4, CH, D), BF16),
        ((3 * FQ, D), BF16),
        ((TC, D), BF16),
        ((3, TC, CH), F32),
        ((TC + 8, CH), F32),
        ((TC, CH), F32),
        ((TC, CH), BF16),
        ((TO, D), F32),
        ((TC, D), BF16),
        ((TC, 3 * FQ), F32),
        ((TC, FQ), BF16),
        ((TC, 2 * FQ), BF16),
        ((4, TC, D), F32),
        ((4, TC, D), BF16),
        ((4, 3, TO, D), BF16),
        ((TO, D), F32),
        ((TC, D), BF16),
        ((TC + 8, CH), F32),
        ((3, TC, CH), BF16),
        ((3 * FQ, HALF), BF16),
        ((3 * FQ, HALF), BF16),
        ((3 * FQ, HALF), BF16),
        ((3, 2 * FB, HALF), BF16),
        ((2 * FB, HALF), BF16),
        ((3, 2 * FB, 128), BF16),
        ((3 * FB, 128), BF16),
        ((3, FQ, 128), BF16),
        ((FQ, 128), BF16),
        ((3, FB, 128), BF16),
        ((4, CH, HALF), BF16),
        ((4, CH, HALF), BF16),
        ((4, CH, HALF), BF16),
        ((3, 4, CB, HALF), BF16),
        ((4, CB, HALF), BF16),
        ((3, 4, CB, 128), BF16),
        ((4, CB, 128), BF16),
        ((8, D), F32),
        ((7, 8, D), F32),
        ((4, 8, D), F32),
        ((4, 8, D), F32),
        ((TO, D), BF16),
        ((TO, D), F32),
    ]
    results = pl.pallas_call(
        kernel,
        out_shape=(
            shape((128, HALF), BF16),
            shape((128, HALF), F32),
            shape((4, CB, HALF), BF16),
            shape((3 * FB, HALF), BF16),
            shape((8, D), F32),
        ),
        in_specs=[whole] * 2 + [vmem] * 4 + [whole] * 7,
        out_specs=(whole,) * 4 + (vmem,),
        scratch_shapes=[pltpu.VMEM(s, t) for s, t in scratch]
        + [
            pltpu.SemaphoreType.DMA((COPIES,)),
            pltpu.SemaphoreType.DMA((COPIES,)),
            pltpu.SemaphoreType.DMA((10,)),
        ],
        compiler_params=pltpu.CompilerParams(
            collective_id=0, has_side_effects=True, vmem_limit_bytes=62 * 2**20
        ),
    )(
        hidden_in,
        cotangent,
        ids,
        first_gain[None],
        second_gain[None],
        taps,
        mixer_b.T,
        mixer_c.T,
        mixer_v.T,
        mixer_out,
        gate_weight.T,
        up_weight.T,
        down_weight,
    )
    copied = [((128, HALF), BF16), ((128, HALF), F32)]
    small_out = [((1, HALF), F32), ((1, HALF), F32), ((3, 32), F32)]
    grads = [((CB, HALF), F32)] * 4 + [((FB, HALF), F32)] * 3
    outs = pl.pallas_call(
        finish,
        out_shape=tuple(shape(a, t) for a, t in copied + grads + small_out),
        in_specs=[vmem] * 5,
        out_specs=(vmem,) * 12,
    )(*results)
    block_out, input_grad, b_g, c_g, v_g, out_g, gate_g, up_g, down_g, first_g, second_g, taps_g = outs
    return (
        block_out,
        input_grad,
        first_g[0],
        b_g.T,
        c_g.T,
        v_g.T,
        taps_g,
        out_g,
        second_g[0],
        gate_g.T,
        up_g.T,
        down_g,
    )


def solution(mesh):
    return jax.shard_map(
        shards,
        mesh=mesh,
        in_specs=(
            P(("dp", "col"), "row"),
            P("dp", None),
            P("row"),
            P("row", "col"),
            P("row", "col"),
            P("row", "col"),
            P(None, "col"),
            P("col", "row"),
            P("row"),
            P("row", "col"),
            P("row", "col"),
            P("col", "row"),
            P(("dp", "col"), "row"),
        ),
        out_specs=(
            P(("dp", "col"), "row"),
            P(("dp", "col"), "row"),
            P("row"),
            P("row", "col"),
            P("row", "col"),
            P("row", "col"),
            P(None, ("col", "row")),
            P("col", "row"),
            P("row"),
            P("row", "col"),
            P("row", "col"),
            P("col", "row"),
        ),
        check_vma=False,
    )
```

```python
import jax
import jax.numpy as jnp
from jax import lax
from jax.experimental import pallas as pl
from jax.experimental.pallas import tpu as pltpu
from jax.sharding import PartitionSpec as P

EPSILON = 1e-05
MESH = pl.DeviceIdType.MESH
F32 = jnp.float32
BF16 = jnp.bfloat16

D = 1024
HALF = 512
CH = 256
CB = 64
FQ = 1152
FB = 288
TC = 256
TO = 64
COPIES = 256


def mod4(value):
    return lax.rem(value + 4, 4)


def nt(a, b):
    return lax.dot_general(a, b, (((1,), (1,)), ((), ())), preferred_element_type=F32)


def nn(a, b):
    return lax.dot_general(a, b, (((1,), (0,)), ((), ())), preferred_element_type=F32)


def tn(a, b):
    return lax.dot_general(a, b, (((0,), (0,)), ((), ())), preferred_element_type=F32)


def loop(count, body):
    def step(i, carry):
        body(i)
        return carry

    lax.fori_loop(0, count, step, 0)


def rows_at(start, size, multiple=32):
    return pl.ds(pl.multiple_of(start, multiple), size)


def lanes_at(start, size):
    return pl.ds(pl.multiple_of(start, 128), size)


def kernel(
    x_in,
    cot_in,
    ids,
    first_in,
    second_in,
    taps_own,
    b_in,
    c_in,
    v_in,
    out_in,
    gate_in,
    up_in,
    down_in,
    block_o,
    input_o,
    mix_o,
    feed_o,
    stats_o,
    small,
    masks,
    xs,
    cs,
    gains,
    taps_in,
    w_mix,
    w_feed,
    fn,
    pre,
    gat,
    cvd,
    mx,
    res,
    sn,
    gu,
    hid,
    dg,
    fulls,
    halves,
    recvs,
    rg,
    rh,
    cg,
    dm,
    go_f,
    cr_f,
    s_f,
    zr_f,
    xs_f,
    xr_f,
    xf_f,
    x1_d,
    t_d,
    z2_d,
    go_m,
    cr_m,
    s_m,
    zr_m,
    xs_m,
    xr_m,
    xf_m,
    st,
    st_y,
    st_z,
    st_x,
    bo_own,
    ig_own,
    ss,
    rs,
    ls,
):
    x = lax.axis_index("dp")
    r = lax.axis_index("row")
    col = lax.axis_index("col")
    z = lax.div(col, 4)
    y = lax.rem(col, 4)
    other = 1 - r
    own_lanes = lanes_at(r * HALF, HALF)
    other_lanes = lanes_at(other * HALF, HALF)
    own_rows = rows_at(y * TO, TO)

    def y_peer(d):
        return (x, r, z * 4 + mod4(y + d))

    def z_peer(d):
        return (x, r, mod4(z + d) * 4 + y)

    def x_peer(d):
        return (mod4(x + d), r, col)

    partner = (x, other, col)
    successor = (x, other, mod4(z + r) * 4 + y)
    predecessor = (x, other, mod4(z + r + 3) * 4 + y)
    halo_extra = (x, other, mod4(z + 2 * r - 1) * 4 + y)

    barrier = pltpu.get_barrier_semaphore()
    greeted = [partner, halo_extra]
    for d in (1, 2, 3):
        greeted += [y_peer(d), (x, other, z * 4 + mod4(y + d)), z_peer(d), x_peer(d)]
    for device in greeted:
        pl.semaphore_signal(barrier, inc=1, device_id=device, device_id_type=MESH)
    pl.semaphore_wait(barrier, len(greeted))

    used = [0]
    sent = []

    def slot(count=1):
        first = used[0]
        used[0] += count
        return first

    def push(source, target, device, index=None):
        i = slot() if index is None else index
        copy = pltpu.make_async_remote_copy(
            src_ref=source,
            dst_ref=target,
            send_sem=ss.at[i],
            recv_sem=rs.at[i],
            device_id=device,
            device_id_type=MESH,
        )
        copy.start()
        sent.append((None, copy))
        return copy

    def place(source, target, device, send_index, recv_index, here):
        copy = pltpu.make_async_remote_copy(
            src_ref=source,
            dst_ref=target,
            send_sem=ss.at[send_index],
            recv_sem=rs.at[recv_index],
            device_id=device,
            device_id_type=MESH,
        )

        @pl.when(here)
        def _():
            pltpu.make_async_copy(source, target, rs.at[recv_index]).start()

        @pl.when(jnp.logical_not(here))
        def _():
            copy.start()

        sent.append((here, copy))

    def arrived(source, target, index):
        pltpu.make_async_remote_copy(
            src_ref=source,
            dst_ref=target,
            send_sem=ss.at[index],
            recv_sem=rs.at[index],
            device_id=partner,
            device_id_type=MESH,
        ).wait_recv()

    def tokens_start(source, target):
        base = slot(4)
        core = lax.div(y, 2)
        block = lax.rem(y, 2)
        region = target.at[rows_at(block * 128, 128), own_lanes]
        for d in (1, 3, 2, 0):
            device = (x, core, z * 4 + mod4(y + d))
            index = base + block * 2 + r
            if d:
                copy = pltpu.make_async_remote_copy(
                    src_ref=source,
                    dst_ref=region,
                    send_sem=ss.at[base + d],
                    recv_sem=rs.at[index],
                    device_id=device,
                    device_id_type=MESH,
                )
                copy.start()
                sent.append((None, copy))
            else:
                place(source, region, device, base, index, core == r)
        return base

    def tokens_finish(source, target, base):
        for s in range(4):
            region = target.at[pl.ds((s // 2) * 128, 128), pl.ds((s % 2) * HALF, HALF)]
            arrived(source, region, base + s)

    def owners_start(source, target):
        base = slot(2)
        chip = 2 * r + lax.div(y, 2)
        region = target.at[rows_at(lax.rem(y, 2) * TO, TO)]
        for core in range(2):
            here = jnp.logical_and(chip == y, r == core)
            place(
                source.at[:, pl.ds(core * HALF, HALF)],
                region,
                (x, core, z * 4 + chip),
                base + core,
                base + lax.rem(y, 2),
                here,
            )
        return base

    def owners_finish(source, target, base):
        for s in range(2):
            arrived(source.at[:, pl.ds(0, HALF)], target.at[pl.ds(s * TO, TO)], base + s)

    local = [0]

    class Section:
        def __init__(self, source, region):
            self.source = source
            self.region = region

        def start(self):
            self.z = {d: push(self.source, self.region(z, r), z_peer(d)) for d in (1, 3, 2)}
            self.mine = pltpu.make_async_copy(self.source, self.region(z, r), ls.at[local[0]])
            local[0] += 1
            self.mine.start()
            self.cross = [push(self.source, self.region(z, r), partner)]

        def forward(self):
            for d in (1, 3, 2):
                self.z[d].wait_recv()
                region = self.region(mod4(z - d), r)
                self.cross.append(push(region, region, partner))

        def finish(self):
            self.mine.wait()
            for copy in self.cross:
                copy.wait_recv()

    class Split:
        def __init__(self, source, region):
            self.source = source
            self.region = region

        def start(self):
            quarter = self.source.at[:, lanes_at(x * 128, 128)]
            self.z = {
                d: push(quarter, self.region(z, r * HALF + x * 128, 128), z_peer(d))
                for d in (1, 3, 2)
            }
            whole = self.region(z, r * HALF, HALF)
            self.mine = pltpu.make_async_copy(self.source, whole, ls.at[local[0]])
            local[0] += 1
            self.mine.start()
            self.cross = [push(self.source, whole, partner)]

        def forward(self):
            self.x = []
            for d in (1, 3, 2):
                self.z[d].wait_recv()
                region = self.region(mod4(z - d), r * HALF + x * 128, 128)
                self.x += [push(region, region, x_peer(e)) for e in (1, 3, 2)]

        def across(self):
            for copy in self.x:
                copy.wait_recv()
            for d in (1, 3, 2):
                region = self.region(mod4(z - d), r * HALF, HALF)
                self.cross.append(push(region, region, partner))

        def finish(self):
            self.mine.wait()
            for copy in self.cross:
                copy.wait_recv()

    def mix_section(s, source):
        return Section(
            source, lambda zz, rr: w_mix.at[s, rows_at(zz * CB, CB), lanes_at(rr * HALF, HALF)]
        )

    mix = [mix_section(s, source) for s, source in enumerate((b_in, c_in, v_in, out_in))]
    gate = Section(
        gate_in, lambda zz, rr: w_feed.at[rows_at(zz * FB, FB), lanes_at(rr * HALF, HALF)]
    )
    up = Split(
        up_in, lambda zz, at, size: w_feed.at[rows_at(FQ + zz * FB, FB), lanes_at(at, size)]
    )
    down = Split(
        down_in,
        lambda zz, at, size: w_feed.at[rows_at(2 * FQ + zz * FB, FB), lanes_at(at, size)],
    )

    def scatter_start(k):
        return [
            push(halves.at[k, rows_at(mod4(y + d) * TO, TO)], recvs.at[k, d - 1], y_peer(d))
            for d in (1, 3, 2)
        ]

    def scatter_finish(k, copies):
        for copy in copies:
            copy.wait_recv()
        total = fulls[k, own_rows, :]
        for d in range(3):
            total = total + recvs[k, d].astype(F32)
        return total

    def gather_start(buffer):
        return [push(buffer.at[own_rows], buffer.at[own_rows], y_peer(d)) for d in (1, 3, 2)]

    def wait(copies):
        for copy in copies:
            copy.wait_recv()

    def product(k, value):
        def body(n):
            lanes = lanes_at(n * 256, 256)
            part = value(lanes)
            fulls[k, :, lanes] = part
            halves[k, :, lanes] = part.astype(BF16)

        loop(4, body)

    small[0:1, :] = first_in[...]
    small[1:2, :] = second_in[...]
    small[2:5, 0:CH] = taps_own[...]
    x_base = tokens_start(x_in, xs)
    for section in mix:
        section.start()
    up.start()
    small_copies = [push(small, gains.at[:, own_lanes], partner)]
    small_copies += [push(small, taps_in.at[d - 1], z_peer(d)) for d in (1, 3, 2)]
    gains[:, own_lanes] = small[...]
    st[...] = jnp.zeros((8, D), F32)
    here = ids[2 : 2 + TC, :]
    for k, first in enumerate((1, 0, 3, 4)):
        masks[k] = (ids[first : first + TC, :] == here).astype(F32)

    tokens_finish(x_in, xs, x_base)
    wait(small_copies)
    cot_base = tokens_start(cot_in, cs)
    first_gain = gains[0:1, :]
    second_gain = gains[1:2, :]
    taps = small[2:5, 0:CH]
    for d in range(3):
        taps = taps + taps_in[d, 2:5, 0:CH]

    def norm_body(i):
        rows = rows_at(i * 32, 32)
        value = xs[rows, :].astype(F32)
        scale = lax.rsqrt(jnp.sum(value * value, axis=1, keepdims=True) / D + EPSILON)
        fn[rows, :] = (value * scale * first_gain).astype(BF16)

    loop(8, norm_body)

    for section in mix:
        section.forward()
    up.forward()
    for section in mix:
        section.finish()

    def pre_body(s):
        pre[s] = nt(fn[...], w_mix[s])

    loop(3, pre_body)

    gat[8 : 8 + TC, :] = pre[0] * pre[2]
    halo = push(gat.at[pl.ds(TC, 8)], gat.at[pl.ds(0, 8)], successor)
    halo.wait_recv()
    down.start()
    gate.start()
    m1 = masks[0, :, 0:1]
    m2 = masks[1, :, 0:1]
    cvd[...] = (
        taps[0:1] * gat[8 : 8 + TC, :]
        + taps[1:2] * (m1 * gat[7 : 7 + TC, :])
        + taps[2:3] * (m2 * gat[6 : 6 + TC, :])
    )
    mx[...] = (pre[1] * cvd[...]).astype(BF16)
    product(0, lambda lanes: nn(mx[...], w_mix[3, :, lanes]))
    first_scatter = scatter_start(0)
    down.forward()

    residual = xs[own_rows, :].astype(F32) + scatter_finish(0, first_scatter)
    res[...] = residual
    second_scale = lax.rsqrt(jnp.sum(residual * residual, axis=1, keepdims=True) / D + EPSILON)
    sn[own_rows, :] = (residual * second_scale * second_gain).astype(BF16)
    sn_copies = gather_start(sn)

    gate.forward()
    up.across()
    tokens_finish(cot_in, cs, cot_base)
    gate.finish()
    up.finish()
    wait(sn_copies)

    def gu_body(n):
        at = n * 256
        gu[:, lanes_at(at, 256)] = nt(sn[...], w_feed[rows_at(at, 256), :])

    loop(9, gu_body)

    down.across()

    def hidden_body(i):
        rows = rows_at(i * 32, 32)
        g = gu[rows, 0:FQ]
        hid[rows, :] = (g * jax.nn.sigmoid(g) * gu[rows, FQ : 2 * FQ]).astype(BF16)

    loop(8, hidden_body)
    down.finish()

    def hg_body(n):
        at = n * 384
        gu[:, lanes_at(2 * FQ + at, 384)] = nt(cs[...], w_feed[rows_at(2 * FQ + at, 384), :])

    loop(3, hg_body)

    def delta_body(i):
        rows = rows_at(i * 32, 32)
        g = gu[rows, 0:FQ]
        u = gu[rows, FQ : 2 * FQ]
        hg = gu[rows, 2 * FQ : 3 * FQ]
        s = jax.nn.sigmoid(g)
        dg[rows, 0:FQ] = (hg * u * s * (1.0 + g * (1.0 - s))).astype(BF16)
        dg[rows, FQ : 2 * FQ] = (hg * (g * s)).astype(BF16)

    loop(8, delta_body)
    product(2, lambda lanes: nn(dg[...], w_feed[0 : 2 * FQ, lanes]))
    grad_scatter = scatter_start(2)
    def go_gu_body(n):
        at = n * 384
        go_f[rows_at(at, 384), :] = tn(dg[:, lanes_at(at, 384)], sn[:, other_lanes]).astype(BF16)

    def go_d_body(n):
        at = n * 384
        go_f[rows_at(2 * FQ + at, 384), :] = tn(
            hid[:, lanes_at(at, 384)], cs[:, other_lanes]
        ).astype(BF16)

    loop(6, go_gu_body)
    cross_gu = push(go_f.at[pl.ds(0, 2 * FQ)], cr_f.at[pl.ds(0, 2 * FQ)], partner)
    loop(3, go_d_body)
    cross_d = push(go_f.at[pl.ds(2 * FQ, FQ)], cr_f.at[pl.ds(2 * FQ, FQ)], partner)

    cross_gu.wait_recv()

    def s_gu_body(n):
        at = n * 384
        rows = rows_at(at, 384)
        s_f[rows, :] = (
            tn(dg[:, lanes_at(at, 384)], sn[:, own_lanes]) + cr_f[rows, :].astype(F32)
        ).astype(BF16)

    loop(6, s_gu_body)

    def feed_send(part):
        return [
            push(
                s_f.at[rows_at(part * FQ + mod4(z + d) * FB, FB)],
                zr_f.at[d - 1, pl.ds(part * FB, FB)],
                z_peer(d),
            )
            for d in (1, 3, 2)
        ]

    feed_z = feed_send(0) + feed_send(1)
    second_grad = scatter_finish(2, grad_scatter)
    residual = res[...]
    second_scale = lax.rsqrt(jnp.sum(residual * residual, axis=1, keepdims=True) / D + EPSILON)
    st[1:2, :] = jnp.sum(second_grad * residual * second_scale, axis=0, keepdims=True)
    weighted = second_grad * second_gain
    cube = second_scale * second_scale * second_scale
    residual_grad = (
        cs[own_rows, :].astype(F32)
        + second_scale * weighted
        - residual * cube * (jnp.sum(weighted * residual, axis=1, keepdims=True) / D)
    )
    rg[...] = residual_grad
    rh[own_rows, :] = residual_grad.astype(BF16)
    rh_copies = gather_start(rh)

    cross_d.wait_recv()

    def s_d_body(n):
        at = n * 384
        rows = rows_at(2 * FQ + at, 384)
        s_f[rows, :] = (
            tn(hid[:, lanes_at(at, 384)], cs[:, own_lanes]) + cr_f[rows, :].astype(F32)
        ).astype(BF16)

    loop(3, s_d_body)
    down_x = [
        push(s_f.at[pl.ds(2 * FQ, FQ), lanes_at(mod4(x + d) * 128, 128)], x1_d.at[d - 1], x_peer(d))
        for d in (1, 3, 2)
    ]
    product(1, lambda lanes: nn(hid[...], w_feed[2 * FQ : 3 * FQ, lanes]))
    block_scatter = scatter_start(1)

    wait(rh_copies)
    mixed_grad = nt(rh[...], w_mix[3])
    cg[0:TC, :] = mixed_grad * pre[1]
    halo_back = push(cg.at[pl.ds(0, 8)], cg.at[pl.ds(TC, 8)], predecessor)
    dm[1] = (mixed_grad * cvd[...]).astype(BF16)

    go_m[3] = tn(mx[...], rh[:, other_lanes]).astype(BF16)

    conv_grad = cg[0:TC, :]
    tap_lanes = lanes_at(y * CH, CH)
    st[2:3, tap_lanes] = jnp.sum(conv_grad * gat[8 : 8 + TC, :], axis=0, keepdims=True)
    st[3:4, tap_lanes] = jnp.sum(conv_grad * m1 * gat[7 : 7 + TC, :], axis=0, keepdims=True)
    st[4:5, tap_lanes] = jnp.sum(conv_grad * m2 * gat[6 : 6 + TC, :], axis=0, keepdims=True)
    halo_back.wait_recv()
    gated_grad = (
        taps[0:1] * conv_grad
        + taps[1:2] * (masks[2, :, 0:1] * cg[1 : 1 + TC, :])
        + taps[2:3] * (masks[3, :, 0:1] * cg[2 : 2 + TC, :])
    )
    dm[0] = (gated_grad * pre[2]).astype(BF16)
    dm[2] = (gated_grad * pre[0]).astype(BF16)

    def first_part(lanes):
        part = nn(dm[0], w_mix[0, :, lanes])
        part = part + nn(dm[1], w_mix[1, :, lanes])
        return part + nn(dm[2], w_mix[2, :, lanes])

    product(3, first_part)
    first_scatter = scatter_start(3)

    def go_m_body(s):
        go_m[s] = tn(dm[s], fn[:, other_lanes]).astype(BF16)

    loop(3, go_m_body)
    cross_m = push(go_m, cr_m, partner)

    x_lanes = lanes_at(x * 128, 128)
    wait(down_x)
    mine = s_f[2 * FQ : 3 * FQ, x_lanes].astype(F32)
    for d in range(3):
        mine = mine + x1_d[d].astype(F32)
    t_d[...] = mine.astype(BF16)
    down_z = [
        push(t_d.at[rows_at(mod4(z + d) * FB, FB)], z2_d.at[d - 1], z_peer(d)) for d in (1, 3, 2)
    ]

    wait(feed_z)
    for part in range(2):
        mine = s_f[rows_at(part * FQ + z * FB, FB), :].astype(F32)
        at = part * FB
        for d in range(3):
            mine = mine + zr_f[d, at : at + FB, :].astype(F32)
        xs_f[at : at + FB, :] = mine.astype(BF16)
    feed_x = [
        push(xs_f.at[:, lanes_at(mod4(x + d) * 128, 128)], xr_f.at[d - 1], x_peer(d))
        for d in (1, 3, 2)
    ]

    cross_m.wait_recv()

    def s_m_body(s):
        s_m[s] = (tn(dm[s], fn[:, own_lanes]) + cr_m[s].astype(F32)).astype(BF16)

    loop(3, s_m_body)
    s_m[3] = (tn(mx[...], rh[:, own_lanes]) + cr_m[3].astype(F32)).astype(BF16)
    mix_z = [
        push(s_m.at[:, rows_at(mod4(z + d) * CB, CB), :], zr_m.at[d - 1], z_peer(d))
        for d in (1, 3, 2)
    ]

    kept = []

    def spread(source, target):
        copy = pltpu.make_async_copy(source, target, ls.at[local[0]])
        local[0] += 1
        copy.start()
        kept.append(copy)
        return [push(source, target, x_peer(d)) for d in (1, 3, 2)]

    wait(down_z)
    mine = t_d[rows_at(z * FB, FB), :].astype(F32)
    for d in range(3):
        mine = mine + z2_d[d].astype(F32)
    xf_f[2 * FB : 3 * FB, :] = mine.astype(BF16)
    down_rows = pl.ds(2 * FB, FB)
    feed_g = spread(xf_f.at[down_rows], feed_o.at[down_rows, x_lanes])

    bo_own[...] = (res[...] + scatter_finish(1, block_scatter)).astype(BF16)
    bo_base = owners_start(bo_own, block_o)

    first_grad = scatter_finish(3, first_scatter)
    value = xs[own_rows, :].astype(F32)
    first_scale = lax.rsqrt(jnp.sum(value * value, axis=1, keepdims=True) / D + EPSILON)
    st[0:1, :] = jnp.sum(first_grad * value * first_scale, axis=0, keepdims=True)
    weighted = first_grad * first_gain
    cube = first_scale * first_scale * first_scale
    ig_own[...] = (
        rg[...]
        + first_scale * weighted
        - value * cube * (jnp.sum(weighted * value, axis=1, keepdims=True) / D)
    )
    ig_base = owners_start(ig_own, input_o)
    stat_copies = [push(st, st_y.at[0], partner)]
    for d in (1, 2, 3):
        stat_copies.append(push(st, st_y.at[2 * d - 1], y_peer(d)))
        stat_copies.append(push(st, st_y.at[2 * d], (x, other, z * 4 + mod4(y + d))))

    wait(feed_x)
    mine = xs_f[:, x_lanes].astype(F32)
    for d in range(3):
        mine = mine + xr_f[d].astype(F32)
    xf_f[0 : 2 * FB, :] = mine.astype(BF16)
    gate_rows = pl.ds(0, 2 * FB)
    feed_g += spread(xf_f.at[gate_rows], feed_o.at[gate_rows, x_lanes])

    wait(stat_copies)
    total = st[...]
    for i in range(7):
        total = total + st_y[i]
    st_z[3] = total
    stat_copies = [push(st_z.at[3], st_z.at[d - 1], z_peer(d)) for d in (1, 3, 2)]

    wait(mix_z)
    mine = s_m[:, rows_at(z * CB, CB), :].astype(F32)
    for d in range(3):
        mine = mine + zr_m[d].astype(F32)
    xs_m[...] = mine.astype(BF16)
    mix_x = [
        push(xs_m.at[:, :, lanes_at(mod4(x + d) * 128, 128)], xr_m.at[d - 1], x_peer(d))
        for d in (1, 3, 2)
    ]
    wait(stat_copies)
    st_x[3] = st_z[0] + st_z[1] + st_z[2] + st_z[3]
    stat_copies = [push(st_x.at[3], st_x.at[d - 1], x_peer(d)) for d in (1, 3, 2)]

    wait(mix_x)
    mine = xs_m[:, :, x_lanes].astype(F32)
    for d in range(3):
        mine = mine + xr_m[d].astype(F32)
    xf_m[...] = mine.astype(BF16)
    mix_g = spread(xf_m, mix_o.at[:, :, x_lanes])

    wait(stat_copies)
    stats_o[...] = st_x[0] + st_x[1] + st_x[2] + st_x[3]
    owners_finish(bo_own, block_o, bo_base)
    owners_finish(ig_own, input_o, ig_base)
    wait(feed_g)
    wait(mix_g)
    for copy in kept:
        copy.wait()

    for here, copy in sent:
        if here is None:
            copy.wait_send()
        else:

            @pl.when(jnp.logical_not(here))
            def _(copy=copy):
                copy.wait_send()


def finish(
    block_i,
    input_i,
    mix_i,
    feed_i,
    stats,
    block_o,
    input_o,
    b_o,
    c_o,
    v_o,
    out_o,
    gate_o,
    up_o,
    down_o,
    first_o,
    second_o,
    taps_o,
):
    r = lax.axis_index("row")
    col = lax.axis_index("col")
    z = lax.div(col, 4)
    y = lax.rem(col, 4)
    block_o[...] = block_i[...]
    input_o[...] = input_i[...]
    lanes = lanes_at(r * HALF, HALF)
    first_o[...] = stats[0:1, lanes]
    second_o[...] = stats[1:2, lanes]
    window = stats[2:5, lanes_at(y * CH + lax.div(z, 2) * 128, 128)]
    place = lax.rem(z, 2) * 2 + r
    total = jnp.zeros((3, 32), F32)
    for k in range(4):
        total = total + jnp.where(place == k, window[:, k * 32 : (k + 1) * 32], 0.0)
    taps_o[...] = total
    for part, target in enumerate((gate_o, up_o, down_o)):
        target[...] = feed_i[part * FB : (part + 1) * FB, :].astype(F32)
    for part, target in enumerate((b_o, c_o, v_o, out_o)):
        target[...] = mix_i[part].astype(F32)


def shards(
    hidden_in,
    segment_ids,
    first_gain,
    mixer_b,
    mixer_c,
    mixer_v,
    conv_kernel,
    mixer_out,
    second_gain,
    gate_weight,
    up_weight,
    down_weight,
    cotangent,
):
    r = lax.axis_index("row")
    col = lax.axis_index("col")
    z = col // 4
    y = col % 4
    ids = jnp.pad(segment_ids[0], ((2, 6),), constant_values=-1)
    ids = lax.dynamic_slice_in_dim(ids, z * 512 + r * TC, TC + 8, 0)
    ids = jnp.broadcast_to(ids[:, None], (TC + 8, 128))
    at_z = lax.broadcasted_iota(jnp.int32, (3, CH), 1) // CB == z
    taps = jnp.where(at_z, jnp.tile(conv_kernel, (1, CH // CB)), 0.0)
    vmem = pl.BlockSpec(memory_space=pltpu.VMEM)
    whole = pl.BlockSpec(memory_space=pl.ANY)
    shape = jax.ShapeDtypeStruct
    scratch = [
        ((8, HALF), F32),
        ((4, TC, 128), F32),
        ((TC, D), BF16),
        ((TC, D), BF16),
        ((8, D), F32),
        ((3, 8, HALF), F32),
        ((4, CH, D), BF16),
        ((3 * FQ, D), BF16),
        ((TC, D), BF16),
        ((3, TC, CH), F32),
        ((TC + 8, CH), F32),
        ((TC, CH), F32),
        ((TC, CH), BF16),
        ((TO, D), F32),
        ((TC, D), BF16),
        ((TC, 3 * FQ), F32),
        ((TC, FQ), BF16),
        ((TC, 2 * FQ), BF16),
        ((4, TC, D), F32),
        ((4, TC, D), BF16),
        ((4, 3, TO, D), BF16),
        ((TO, D), F32),
        ((TC, D), BF16),
        ((TC + 8, CH), F32),
        ((3, TC, CH), BF16),
        ((3 * FQ, HALF), BF16),
        ((3 * FQ, HALF), BF16),
        ((3 * FQ, HALF), BF16),
        ((3, 2 * FB, HALF), BF16),
        ((2 * FB, HALF), BF16),
        ((3, 2 * FB, 128), BF16),
        ((3 * FB, 128), BF16),
        ((3, FQ, 128), BF16),
        ((FQ, 128), BF16),
        ((3, FB, 128), BF16),
        ((4, CH, HALF), BF16),
        ((4, CH, HALF), BF16),
        ((4, CH, HALF), BF16),
        ((3, 4, CB, HALF), BF16),
        ((4, CB, HALF), BF16),
        ((3, 4, CB, 128), BF16),
        ((4, CB, 128), BF16),
        ((8, D), F32),
        ((7, 8, D), F32),
        ((4, 8, D), F32),
        ((4, 8, D), F32),
        ((TO, D), BF16),
        ((TO, D), F32),
    ]
    results = pl.pallas_call(
        kernel,
        out_shape=(
            shape((128, HALF), BF16),
            shape((128, HALF), F32),
            shape((4, CB, HALF), BF16),
            shape((3 * FB, HALF), BF16),
            shape((8, D), F32),
        ),
        in_specs=[whole] * 2 + [vmem] * 4 + [whole] * 7,
        out_specs=(whole,) * 4 + (vmem,),
        scratch_shapes=[pltpu.VMEM(s, t) for s, t in scratch]
        + [
            pltpu.SemaphoreType.DMA((COPIES,)),
            pltpu.SemaphoreType.DMA((COPIES,)),
            pltpu.SemaphoreType.DMA((10,)),
        ],
        compiler_params=pltpu.CompilerParams(
            collective_id=0, has_side_effects=True, vmem_limit_bytes=62 * 2**20
        ),
    )(
        hidden_in,
        cotangent,
        ids,
        first_gain[None],
        second_gain[None],
        taps,
        mixer_b.T,
        mixer_c.T,
        mixer_v.T,
        mixer_out,
        gate_weight.T,
        up_weight.T,
        down_weight,
    )
    copied = [((128, HALF), BF16), ((128, HALF), F32)]
    small_out = [((1, HALF), F32), ((1, HALF), F32), ((3, 32), F32)]
    grads = [((CB, HALF), F32)] * 4 + [((FB, HALF), F32)] * 3
    outs = pl.pallas_call(
        finish,
        out_shape=tuple(shape(a, t) for a, t in copied + grads + small_out),
        in_specs=[vmem] * 5,
        out_specs=(vmem,) * 12,
    )(*results)
    block_out, input_grad, b_g, c_g, v_g, out_g, gate_g, up_g, down_g, first_g, second_g, taps_g = outs
    return (
        block_out,
        input_grad,
        first_g[0],
        b_g.T,
        c_g.T,
        v_g.T,
        taps_g,
        out_g,
        second_g[0],
        gate_g.T,
        up_g.T,
        down_g,
    )


def solution(mesh):
    return jax.shard_map(
        shards,
        mesh=mesh,
        in_specs=(
            P(("dp", "col"), "row"),
            P("dp", None),
            P("row"),
            P("row", "col"),
            P("row", "col"),
            P("row", "col"),
            P(None, "col"),
            P("col", "row"),
            P("row"),
            P("row", "col"),
            P("row", "col"),
            P("col", "row"),
            P(("dp", "col"), "row"),
        ),
        out_specs=(
            P(("dp", "col"), "row"),
            P(("dp", "col"), "row"),
            P("row"),
            P("row", "col"),
            P("row", "col"),
            P("row", "col"),
            P(None, ("col", "row")),
            P("col", "row"),
            P("row"),
            P("row", "col"),
            P("row", "col"),
            P("col", "row"),
        ),
        check_vma=False,
    )
```

```python
import jax
import jax.numpy as jnp
from jax import lax
from jax.experimental import pallas as pl
from jax.experimental.pallas import tpu as pltpu
from jax.sharding import PartitionSpec as P

EPSILON = 1e-05
MESH = pl.DeviceIdType.MESH
F32 = jnp.float32
BF16 = jnp.bfloat16

D = 1024
HALF = 512
CH = 256
CB = 64
FQ = 1152
FB = 288
TC = 256
TO = 64
COPIES = 256


def mod4(value):
    return lax.rem(value + 4, 4)


def nt(a, b):
    return lax.dot_general(a, b, (((1,), (1,)), ((), ())), preferred_element_type=F32)


def nn(a, b):
    return lax.dot_general(a, b, (((1,), (0,)), ((), ())), preferred_element_type=F32)


def tn(a, b):
    return lax.dot_general(a, b, (((0,), (0,)), ((), ())), preferred_element_type=F32)


def loop(count, body):
    def step(i, carry):
        body(i)
        return carry

    lax.fori_loop(0, count, step, 0)


def rows_at(start, size, multiple=32):
    return pl.ds(pl.multiple_of(start, multiple), size)


def lanes_at(start, size):
    return pl.ds(pl.multiple_of(start, 128), size)


def kernel(
    x_in,
    cot_in,
    ids,
    first_in,
    second_in,
    taps_own,
    b_in,
    c_in,
    v_in,
    out_in,
    gate_in,
    up_in,
    down_in,
    block_o,
    input_o,
    mix_o,
    feed_o,
    stats_o,
    small,
    masks,
    xs,
    cs,
    gains,
    taps_in,
    w_mix,
    w_feed,
    fn,
    pre,
    gat,
    cvd,
    mx,
    res,
    sn,
    gu,
    hid,
    dg,
    fulls,
    halves,
    recvs,
    rg,
    rh,
    cg,
    dm,
    go_f,
    cr_f,
    s_f,
    zr_f,
    xs_f,
    xr_f,
    xf_f,
    x1_d,
    t_d,
    z2_d,
    go_m,
    cr_m,
    s_m,
    zr_m,
    xs_m,
    xr_m,
    xf_m,
    st,
    st_y,
    st_z,
    st_x,
    bo_own,
    ig_own,
    ss,
    rs,
    ls,
):
    x = lax.axis_index("dp")
    r = lax.axis_index("row")
    col = lax.axis_index("col")
    z = lax.div(col, 4)
    y = lax.rem(col, 4)
    other = 1 - r
    own_lanes = lanes_at(r * HALF, HALF)
    other_lanes = lanes_at(other * HALF, HALF)
    own_rows = rows_at(y * TO, TO)

    def y_peer(d):
        return (x, r, z * 4 + mod4(y + d))

    def z_peer(d):
        return (x, r, mod4(z + d) * 4 + y)

    def x_peer(d):
        return (mod4(x + d), r, col)

    partner = (x, other, col)
    successor = (x, other, mod4(z + r) * 4 + y)
    predecessor = (x, other, mod4(z + r + 3) * 4 + y)
    halo_extra = (x, other, mod4(z + 2 * r - 1) * 4 + y)

    barrier = pltpu.get_barrier_semaphore()
    greeted = [partner, halo_extra]
    for d in (1, 2, 3):
        greeted += [y_peer(d), (x, other, z * 4 + mod4(y + d)), z_peer(d), x_peer(d)]
    for device in greeted:
        pl.semaphore_signal(barrier, inc=1, device_id=device, device_id_type=MESH)
    pl.semaphore_wait(barrier, len(greeted))

    used = [0]
    sent = []

    def slot(count=1):
        first = used[0]
        used[0] += count
        return first

    def push(source, target, device, index=None):
        i = slot() if index is None else index
        copy = pltpu.make_async_remote_copy(
            src_ref=source,
            dst_ref=target,
            send_sem=ss.at[i],
            recv_sem=rs.at[i],
            device_id=device,
            device_id_type=MESH,
        )
        copy.start()
        sent.append((None, copy))
        return copy

    def place(source, target, device, send_index, recv_index, here):
        copy = pltpu.make_async_remote_copy(
            src_ref=source,
            dst_ref=target,
            send_sem=ss.at[send_index],
            recv_sem=rs.at[recv_index],
            device_id=device,
            device_id_type=MESH,
        )

        @pl.when(here)
        def _():
            pltpu.make_async_copy(source, target, rs.at[recv_index]).start()

        @pl.when(jnp.logical_not(here))
        def _():
            copy.start()

        sent.append((here, copy))

    def arrived(source, target, index):
        pltpu.make_async_remote_copy(
            src_ref=source,
            dst_ref=target,
            send_sem=ss.at[index],
            recv_sem=rs.at[index],
            device_id=partner,
            device_id_type=MESH,
        ).wait_recv()

    def tokens_start(source, target):
        base = slot(4)
        core = lax.div(y, 2)
        block = lax.rem(y, 2)
        region = target.at[rows_at(block * 128, 128), own_lanes]
        for d in (1, 3, 2, 0):
            device = (x, core, z * 4 + mod4(y + d))
            index = base + block * 2 + r
            if d:
                copy = pltpu.make_async_remote_copy(
                    src_ref=source,
                    dst_ref=region,
                    send_sem=ss.at[base + d],
                    recv_sem=rs.at[index],
                    device_id=device,
                    device_id_type=MESH,
                )
                copy.start()
                sent.append((None, copy))
            else:
                place(source, region, device, base, index, core == r)
        return base

    def tokens_finish(source, target, base):
        for s in range(4):
            region = target.at[pl.ds((s // 2) * 128, 128), pl.ds((s % 2) * HALF, HALF)]
            arrived(source, region, base + s)

    def owners_start(source, target):
        base = slot(2)
        chip = 2 * r + lax.div(y, 2)
        region = target.at[rows_at(lax.rem(y, 2) * TO, TO)]
        for core in range(2):
            here = jnp.logical_and(chip == y, r == core)
            place(
                source.at[:, pl.ds(core * HALF, HALF)],
                region,
                (x, core, z * 4 + chip),
                base + core,
                base + lax.rem(y, 2),
                here,
            )
        return base

    def owners_finish(source, target, base):
        for s in range(2):
            arrived(source.at[:, pl.ds(0, HALF)], target.at[pl.ds(s * TO, TO)], base + s)

    local = [0]

    class Section:
        def __init__(self, source, region):
            self.source = source
            self.region = region

        def start(self):
            self.z = {d: push(self.source, self.region(z, r), z_peer(d)) for d in (1, 3, 2)}
            self.mine = pltpu.make_async_copy(self.source, self.region(z, r), ls.at[local[0]])
            local[0] += 1
            self.mine.start()
            self.cross = [push(self.source, self.region(z, r), partner)]

        def forward(self):
            for d in (1, 3, 2):
                self.z[d].wait_recv()
                region = self.region(mod4(z - d), r)
                self.cross.append(push(region, region, partner))

        def finish(self):
            self.mine.wait()
            for copy in self.cross:
                copy.wait_recv()

    class Split:
        def __init__(self, source, region):
            self.source = source
            self.region = region

        def start(self):
            quarter = self.source.at[:, lanes_at(x * 128, 128)]
            self.z = {
                d: push(quarter, self.region(z, r * HALF + x * 128, 128), z_peer(d))
                for d in (1, 3, 2)
            }
            whole = self.region(z, r * HALF, HALF)
            self.mine = pltpu.make_async_copy(self.source, whole, ls.at[local[0]])
            local[0] += 1
            self.mine.start()
            self.cross = [push(self.source, whole, partner)]

        def forward(self):
            self.x = []
            for d in (1, 3, 2):
                self.z[d].wait_recv()
                region = self.region(mod4(z - d), r * HALF + x * 128, 128)
                self.x += [push(region, region, x_peer(e)) for e in (1, 3, 2)]

        def across(self):
            for copy in self.x:
                copy.wait_recv()
            for d in (1, 3, 2):
                region = self.region(mod4(z - d), r * HALF, HALF)
                self.cross.append(push(region, region, partner))

        def finish(self):
            self.mine.wait()
            for copy in self.cross:
                copy.wait_recv()

    def mix_section(s, source):
        return Section(
            source, lambda zz, rr: w_mix.at[s, rows_at(zz * CB, CB), lanes_at(rr * HALF, HALF)]
        )

    mix = [mix_section(s, source) for s, source in enumerate((b_in, c_in, v_in, out_in))]
    gate = Section(
        gate_in, lambda zz, rr: w_feed.at[rows_at(zz * FB, FB), lanes_at(rr * HALF, HALF)]
    )
    up = Split(
        up_in, lambda zz, at, size: w_feed.at[rows_at(FQ + zz * FB, FB), lanes_at(at, size)]
    )
    down = Split(
        down_in,
        lambda zz, at, size: w_feed.at[rows_at(2 * FQ + zz * FB, FB), lanes_at(at, size)],
    )

    def scatter_start(k):
        return [
            push(halves.at[k, rows_at(mod4(y + d) * TO, TO)], recvs.at[k, d - 1], y_peer(d))
            for d in (1, 3, 2)
        ]

    def scatter_finish(k, copies):
        for copy in copies:
            copy.wait_recv()
        total = fulls[k, own_rows, :]
        for d in range(3):
            total = total + recvs[k, d].astype(F32)
        return total

    def gather_start(buffer):
        return [push(buffer.at[own_rows], buffer.at[own_rows], y_peer(d)) for d in (1, 3, 2)]

    def wait(copies):
        for copy in copies:
            copy.wait_recv()

    def product(k, value):
        def body(n):
            lanes = lanes_at(n * 256, 256)
            part = value(lanes)
            fulls[k, :, lanes] = part
            halves[k, :, lanes] = part.astype(BF16)

        loop(4, body)

    small[0:1, :] = first_in[...]
    small[1:2, :] = second_in[...]
    small[2:5, 0:CH] = taps_own[...]
    x_base = tokens_start(x_in, xs)
    for section in mix:
        section.start()
    up.start()
    small_copies = [push(small, gains.at[:, own_lanes], partner)]
    small_copies += [push(small, taps_in.at[d - 1], z_peer(d)) for d in (1, 3, 2)]
    gains[:, own_lanes] = small[...]
    st[...] = jnp.zeros((8, D), F32)
    here = ids[2 : 2 + TC, :]
    for k, first in enumerate((1, 0, 3, 4)):
        masks[k] = (ids[first : first + TC, :] == here).astype(F32)

    tokens_finish(x_in, xs, x_base)
    wait(small_copies)
    cot_base = tokens_start(cot_in, cs)
    first_gain = gains[0:1, :]
    second_gain = gains[1:2, :]
    taps = small[2:5, 0:CH]
    for d in range(3):
        taps = taps + taps_in[d, 2:5, 0:CH]

    def norm_body(i):
        rows = rows_at(i * 32, 32)
        value = xs[rows, :].astype(F32)
        scale = lax.rsqrt(jnp.sum(value * value, axis=1, keepdims=True) / D + EPSILON)
        fn[rows, :] = (value * scale * first_gain).astype(BF16)

    loop(8, norm_body)

    for section in mix:
        section.forward()
    up.forward()
    for section in mix:
        section.finish()

    def pre_body(s):
        pre[s] = nt(fn[...], w_mix[s])

    loop(3, pre_body)

    gat[8 : 8 + TC, :] = pre[0] * pre[2]
    halo = push(gat.at[pl.ds(TC, 8)], gat.at[pl.ds(0, 8)], successor)
    halo.wait_recv()
    down.start()
    gate.start()
    m1 = masks[0, :, 0:1]
    m2 = masks[1, :, 0:1]
    cvd[...] = (
        taps[0:1] * gat[8 : 8 + TC, :]
        + taps[1:2] * (m1 * gat[7 : 7 + TC, :])
        + taps[2:3] * (m2 * gat[6 : 6 + TC, :])
    )
    mx[...] = (pre[1] * cvd[...]).astype(BF16)
    product(0, lambda lanes: nn(mx[...], w_mix[3, :, lanes]))
    first_scatter = scatter_start(0)
    down.forward()

    residual = xs[own_rows, :].astype(F32) + scatter_finish(0, first_scatter)
    res[...] = residual
    second_scale = lax.rsqrt(jnp.sum(residual * residual, axis=1, keepdims=True) / D + EPSILON)
    sn[own_rows, :] = (residual * second_scale * second_gain).astype(BF16)
    sn_copies = gather_start(sn)

    gate.forward()
    up.across()
    tokens_finish(cot_in, cs, cot_base)
    gate.finish()
    up.finish()
    wait(sn_copies)

    def gu_body(n):
        at = n * 256
        gu[:, lanes_at(at, 256)] = nt(sn[...], w_feed[rows_at(at, 256), :])

    loop(9, gu_body)

    down.across()

    def hidden_body(i):
        rows = rows_at(i * 32, 32)
        g = gu[rows, 0:FQ]
        hid[rows, :] = (g * jax.nn.sigmoid(g) * gu[rows, FQ : 2 * FQ]).astype(BF16)

    loop(8, hidden_body)
    down.finish()

    def hg_body(n):
        at = n * 384
        gu[:, lanes_at(2 * FQ + at, 384)] = nt(cs[...], w_feed[rows_at(2 * FQ + at, 384), :])

    loop(3, hg_body)

    def delta_body(i):
        rows = rows_at(i * 32, 32)
        g = gu[rows, 0:FQ]
        u = gu[rows, FQ : 2 * FQ]
        hg = gu[rows, 2 * FQ : 3 * FQ]
        s = jax.nn.sigmoid(g)
        dg[rows, 0:FQ] = (hg * u * s * (1.0 + g * (1.0 - s))).astype(BF16)
        dg[rows, FQ : 2 * FQ] = (hg * (g * s)).astype(BF16)

    loop(8, delta_body)
    product(2, lambda lanes: nn(dg[...], w_feed[0 : 2 * FQ, lanes]))
    grad_scatter = scatter_start(2)
    def go_gu_body(n):
        at = n * 384
        go_f[rows_at(at, 384), :] = tn(dg[:, lanes_at(at, 384)], sn[:, other_lanes]).astype(BF16)

    def go_d_body(n):
        at = n * 384
        go_f[rows_at(2 * FQ + at, 384), :] = tn(
            hid[:, lanes_at(at, 384)], cs[:, other_lanes]
        ).astype(BF16)

    loop(6, go_gu_body)
    cross_gu = push(go_f.at[pl.ds(0, 2 * FQ)], cr_f.at[pl.ds(0, 2 * FQ)], partner)
    loop(3, go_d_body)
    cross_d = push(go_f.at[pl.ds(2 * FQ, FQ)], cr_f.at[pl.ds(2 * FQ, FQ)], partner)

    cross_gu.wait_recv()

    def s_gu_body(n):
        at = n * 384
        rows = rows_at(at, 384)
        s_f[rows, :] = (
            tn(dg[:, lanes_at(at, 384)], sn[:, own_lanes]) + cr_f[rows, :].astype(F32)
        ).astype(BF16)

    loop(6, s_gu_body)

    def feed_send(part):
        return [
            push(
                s_f.at[rows_at(part * FQ + mod4(z + d) * FB, FB)],
                zr_f.at[d - 1, pl.ds(part * FB, FB)],
                z_peer(d),
            )
            for d in (1, 3, 2)
        ]

    feed_z = feed_send(0)
    second_grad = scatter_finish(2, grad_scatter)
    residual = res[...]
    second_scale = lax.rsqrt(jnp.sum(residual * residual, axis=1, keepdims=True) / D + EPSILON)
    st[1:2, :] = jnp.sum(second_grad * residual * second_scale, axis=0, keepdims=True)
    weighted = second_grad * second_gain
    cube = second_scale * second_scale * second_scale
    residual_grad = (
        cs[own_rows, :].astype(F32)
        + second_scale * weighted
        - residual * cube * (jnp.sum(weighted * residual, axis=1, keepdims=True) / D)
    )
    rg[...] = residual_grad
    rh[own_rows, :] = residual_grad.astype(BF16)
    rh_copies = gather_start(rh)

    cross_d.wait_recv()

    def s_d_body(n):
        at = n * 384
        rows = rows_at(2 * FQ + at, 384)
        s_f[rows, :] = (
            tn(hid[:, lanes_at(at, 384)], cs[:, own_lanes]) + cr_f[rows, :].astype(F32)
        ).astype(BF16)

    loop(3, s_d_body)
    down_x = [
        push(s_f.at[pl.ds(2 * FQ, FQ), lanes_at(mod4(x + d) * 128, 128)], x1_d.at[d - 1], x_peer(d))
        for d in (1, 3, 2)
    ]
    product(1, lambda lanes: nn(hid[...], w_feed[2 * FQ : 3 * FQ, lanes]))
    block_scatter = scatter_start(1)

    wait(rh_copies)
    mixed_grad = nt(rh[...], w_mix[3])
    cg[0:TC, :] = mixed_grad * pre[1]
    halo_back = push(cg.at[pl.ds(0, 8)], cg.at[pl.ds(TC, 8)], predecessor)
    dm[1] = (mixed_grad * cvd[...]).astype(BF16)

    go_m[3] = tn(mx[...], rh[:, other_lanes]).astype(BF16)

    conv_grad = cg[0:TC, :]
    tap_lanes = lanes_at(y * CH, CH)
    st[2:3, tap_lanes] = jnp.sum(conv_grad * gat[8 : 8 + TC, :], axis=0, keepdims=True)
    st[3:4, tap_lanes] = jnp.sum(conv_grad * m1 * gat[7 : 7 + TC, :], axis=0, keepdims=True)
    st[4:5, tap_lanes] = jnp.sum(conv_grad * m2 * gat[6 : 6 + TC, :], axis=0, keepdims=True)
    halo_back.wait_recv()
    feed_z += feed_send(1)
    gated_grad = (
        taps[0:1] * conv_grad
        + taps[1:2] * (masks[2, :, 0:1] * cg[1 : 1 + TC, :])
        + taps[2:3] * (masks[3, :, 0:1] * cg[2 : 2 + TC, :])
    )
    dm[0] = (gated_grad * pre[2]).astype(BF16)
    dm[2] = (gated_grad * pre[0]).astype(BF16)

    def first_part(lanes):
        part = nn(dm[0], w_mix[0, :, lanes])
        part = part + nn(dm[1], w_mix[1, :, lanes])
        return part + nn(dm[2], w_mix[2, :, lanes])

    product(3, first_part)
    first_scatter = scatter_start(3)

    def go_m_body(s):
        go_m[s] = tn(dm[s], fn[:, other_lanes]).astype(BF16)

    loop(3, go_m_body)
    cross_m = push(go_m, cr_m, partner)

    x_lanes = lanes_at(x * 128, 128)
    wait(down_x)
    mine = s_f[2 * FQ : 3 * FQ, x_lanes].astype(F32)
    for d in range(3):
        mine = mine + x1_d[d].astype(F32)
    t_d[...] = mine.astype(BF16)
    down_z = [
        push(t_d.at[rows_at(mod4(z + d) * FB, FB)], z2_d.at[d - 1], z_peer(d)) for d in (1, 3, 2)
    ]

    cross_m.wait_recv()

    def s_m_body(s):
        s_m[s] = (tn(dm[s], fn[:, own_lanes]) + cr_m[s].astype(F32)).astype(BF16)

    loop(3, s_m_body)
    s_m[3] = (tn(mx[...], rh[:, own_lanes]) + cr_m[3].astype(F32)).astype(BF16)
    mix_z = [
        push(s_m.at[:, rows_at(mod4(z + d) * CB, CB), :], zr_m.at[d - 1], z_peer(d))
        for d in (1, 3, 2)
    ]

    wait(feed_z)
    for part in range(2):
        mine = s_f[rows_at(part * FQ + z * FB, FB), :].astype(F32)
        at = part * FB
        for d in range(3):
            mine = mine + zr_f[d, at : at + FB, :].astype(F32)
        xs_f[at : at + FB, :] = mine.astype(BF16)
    feed_x = [
        push(xs_f.at[:, lanes_at(mod4(x + d) * 128, 128)], xr_f.at[d - 1], x_peer(d))
        for d in (1, 3, 2)
    ]

    kept = []

    def spread(source, target):
        copy = pltpu.make_async_copy(source, target, ls.at[local[0]])
        local[0] += 1
        copy.start()
        kept.append(copy)
        return [push(source, target, x_peer(d)) for d in (1, 3, 2)]

    wait(down_z)
    mine = t_d[rows_at(z * FB, FB), :].astype(F32)
    for d in range(3):
        mine = mine + z2_d[d].astype(F32)
    xf_f[2 * FB : 3 * FB, :] = mine.astype(BF16)
    down_rows = pl.ds(2 * FB, FB)
    feed_g = spread(xf_f.at[down_rows], feed_o.at[down_rows, x_lanes])

    bo_own[...] = (res[...] + scatter_finish(1, block_scatter)).astype(BF16)
    bo_base = owners_start(bo_own, block_o)

    first_grad = scatter_finish(3, first_scatter)
    value = xs[own_rows, :].astype(F32)
    first_scale = lax.rsqrt(jnp.sum(value * value, axis=1, keepdims=True) / D + EPSILON)
    st[0:1, :] = jnp.sum(first_grad * value * first_scale, axis=0, keepdims=True)
    weighted = first_grad * first_gain
    cube = first_scale * first_scale * first_scale
    ig_own[...] = (
        rg[...]
        + first_scale * weighted
        - value * cube * (jnp.sum(weighted * value, axis=1, keepdims=True) / D)
    )
    ig_base = owners_start(ig_own, input_o)
    stat_copies = [push(st, st_y.at[0], partner)]
    for d in (1, 2, 3):
        stat_copies.append(push(st, st_y.at[2 * d - 1], y_peer(d)))
        stat_copies.append(push(st, st_y.at[2 * d], (x, other, z * 4 + mod4(y + d))))

    wait(feed_x)
    mine = xs_f[:, x_lanes].astype(F32)
    for d in range(3):
        mine = mine + xr_f[d].astype(F32)
    xf_f[0 : 2 * FB, :] = mine.astype(BF16)
    gate_rows = pl.ds(0, 2 * FB)
    feed_g += spread(xf_f.at[gate_rows], feed_o.at[gate_rows, x_lanes])

    wait(stat_copies)
    total = st[...]
    for i in range(7):
        total = total + st_y[i]
    st_z[3] = total
    stat_copies = [push(st_z.at[3], st_z.at[d - 1], z_peer(d)) for d in (1, 3, 2)]

    wait(mix_z)
    mine = s_m[:, rows_at(z * CB, CB), :].astype(F32)
    for d in range(3):
        mine = mine + zr_m[d].astype(F32)
    xs_m[...] = mine.astype(BF16)
    mix_x = [
        push(xs_m.at[:, :, lanes_at(mod4(x + d) * 128, 128)], xr_m.at[d - 1], x_peer(d))
        for d in (1, 3, 2)
    ]
    wait(stat_copies)
    st_x[3] = st_z[0] + st_z[1] + st_z[2] + st_z[3]
    stat_copies = [push(st_x.at[3], st_x.at[d - 1], x_peer(d)) for d in (1, 3, 2)]

    wait(mix_x)
    mine = xs_m[:, :, x_lanes].astype(F32)
    for d in range(3):
        mine = mine + xr_m[d].astype(F32)
    xf_m[...] = mine.astype(BF16)
    mix_g = spread(xf_m, mix_o.at[:, :, x_lanes])

    wait(stat_copies)
    stats_o[...] = st_x[0] + st_x[1] + st_x[2] + st_x[3]
    owners_finish(bo_own, block_o, bo_base)
    owners_finish(ig_own, input_o, ig_base)
    wait(feed_g)
    wait(mix_g)
    for copy in kept:
        copy.wait()

    for here, copy in sent:
        if here is None:
            copy.wait_send()
        else:

            @pl.when(jnp.logical_not(here))
            def _(copy=copy):
                copy.wait_send()


def finish(
    block_i,
    input_i,
    mix_i,
    feed_i,
    stats,
    block_o,
    input_o,
    b_o,
    c_o,
    v_o,
    out_o,
    gate_o,
    up_o,
    down_o,
    first_o,
    second_o,
    taps_o,
):
    r = lax.axis_index("row")
    col = lax.axis_index("col")
    z = lax.div(col, 4)
    y = lax.rem(col, 4)
    block_o[...] = block_i[...]
    input_o[...] = input_i[...]
    lanes = lanes_at(r * HALF, HALF)
    first_o[...] = stats[0:1, lanes]
    second_o[...] = stats[1:2, lanes]
    window = stats[2:5, lanes_at(y * CH + lax.div(z, 2) * 128, 128)]
    place = lax.rem(z, 2) * 2 + r
    total = jnp.zeros((3, 32), F32)
    for k in range(4):
        total = total + jnp.where(place == k, window[:, k * 32 : (k + 1) * 32], 0.0)
    taps_o[...] = total
    for part, target in enumerate((gate_o, up_o, down_o)):
        target[...] = feed_i[part * FB : (part + 1) * FB, :].astype(F32)
    for part, target in enumerate((b_o, c_o, v_o, out_o)):
        target[...] = mix_i[part].astype(F32)


def shards(
    hidden_in,
    segment_ids,
    first_gain,
    mixer_b,
    mixer_c,
    mixer_v,
    conv_kernel,
    mixer_out,
    second_gain,
    gate_weight,
    up_weight,
    down_weight,
    cotangent,
):
    r = lax.axis_index("row")
    col = lax.axis_index("col")
    z = col // 4
    y = col % 4
    ids = jnp.pad(segment_ids[0], ((2, 6),), constant_values=-1)
    ids = lax.dynamic_slice_in_dim(ids, z * 512 + r * TC, TC + 8, 0)
    ids = jnp.broadcast_to(ids[:, None], (TC + 8, 128))
    at_z = lax.broadcasted_iota(jnp.int32, (3, CH), 1) // CB == z
    taps = jnp.where(at_z, jnp.tile(conv_kernel, (1, CH // CB)), 0.0)
    vmem = pl.BlockSpec(memory_space=pltpu.VMEM)
    whole = pl.BlockSpec(memory_space=pl.ANY)
    shape = jax.ShapeDtypeStruct
    scratch = [
        ((8, HALF), F32),
        ((4, TC, 128), F32),
        ((TC, D), BF16),
        ((TC, D), BF16),
        ((8, D), F32),
        ((3, 8, HALF), F32),
        ((4, CH, D), BF16),
        ((3 * FQ, D), BF16),
        ((TC, D), BF16),
        ((3, TC, CH), F32),
        ((TC + 8, CH), F32),
        ((TC, CH), F32),
        ((TC, CH), BF16),
        ((TO, D), F32),
        ((TC, D), BF16),
        ((TC, 3 * FQ), F32),
        ((TC, FQ), BF16),
        ((TC, 2 * FQ), BF16),
        ((4, TC, D), F32),
        ((4, TC, D), BF16),
        ((4, 3, TO, D), BF16),
        ((TO, D), F32),
        ((TC, D), BF16),
        ((TC + 8, CH), F32),
        ((3, TC, CH), BF16),
        ((3 * FQ, HALF), BF16),
        ((3 * FQ, HALF), BF16),
        ((3 * FQ, HALF), BF16),
        ((3, 2 * FB, HALF), BF16),
        ((2 * FB, HALF), BF16),
        ((3, 2 * FB, 128), BF16),
        ((3 * FB, 128), BF16),
        ((3, FQ, 128), BF16),
        ((FQ, 128), BF16),
        ((3, FB, 128), BF16),
        ((4, CH, HALF), BF16),
        ((4, CH, HALF), BF16),
        ((4, CH, HALF), BF16),
        ((3, 4, CB, HALF), BF16),
        ((4, CB, HALF), BF16),
        ((3, 4, CB, 128), BF16),
        ((4, CB, 128), BF16),
        ((8, D), F32),
        ((7, 8, D), F32),
        ((4, 8, D), F32),
        ((4, 8, D), F32),
        ((TO, D), BF16),
        ((TO, D), F32),
    ]
    results = pl.pallas_call(
        kernel,
        out_shape=(
            shape((128, HALF), BF16),
            shape((128, HALF), F32),
            shape((4, CB, HALF), BF16),
            shape((3 * FB, HALF), BF16),
            shape((8, D), F32),
        ),
        in_specs=[whole] * 2 + [vmem] * 4 + [whole] * 7,
        out_specs=(whole,) * 4 + (vmem,),
        scratch_shapes=[pltpu.VMEM(s, t) for s, t in scratch]
        + [
            pltpu.SemaphoreType.DMA((COPIES,)),
            pltpu.SemaphoreType.DMA((COPIES,)),
            pltpu.SemaphoreType.DMA((10,)),
        ],
        compiler_params=pltpu.CompilerParams(
            collective_id=0, has_side_effects=True, vmem_limit_bytes=62 * 2**20
        ),
    )(
        hidden_in,
        cotangent,
        ids,
        first_gain[None],
        second_gain[None],
        taps,
        mixer_b.T,
        mixer_c.T,
        mixer_v.T,
        mixer_out,
        gate_weight.T,
        up_weight.T,
        down_weight,
    )
    copied = [((128, HALF), BF16), ((128, HALF), F32)]
    small_out = [((1, HALF), F32), ((1, HALF), F32), ((3, 32), F32)]
    grads = [((CB, HALF), F32)] * 4 + [((FB, HALF), F32)] * 3
    outs = pl.pallas_call(
        finish,
        out_shape=tuple(shape(a, t) for a, t in copied + grads + small_out),
        in_specs=[vmem] * 5,
        out_specs=(vmem,) * 12,
    )(*results)
    block_out, input_grad, b_g, c_g, v_g, out_g, gate_g, up_g, down_g, first_g, second_g, taps_g = outs
    return (
        block_out,
        input_grad,
        first_g[0],
        b_g.T,
        c_g.T,
        v_g.T,
        taps_g,
        out_g,
        second_g[0],
        gate_g.T,
        up_g.T,
        down_g,
    )


def solution(mesh):
    return jax.shard_map(
        shards,
        mesh=mesh,
        in_specs=(
            P(("dp", "col"), "row"),
            P("dp", None),
            P("row"),
            P("row", "col"),
            P("row", "col"),
            P("row", "col"),
            P(None, "col"),
            P("col", "row"),
            P("row"),
            P("row", "col"),
            P("row", "col"),
            P("col", "row"),
            P(("dp", "col"), "row"),
        ),
        out_specs=(
            P(("dp", "col"), "row"),
            P(("dp", "col"), "row"),
            P("row"),
            P("row", "col"),
            P("row", "col"),
            P("row", "col"),
            P(None, ("col", "row")),
            P("col", "row"),
            P("row"),
            P("row", "col"),
            P("row", "col"),
            P("col", "row"),
        ),
        check_vma=False,
    )
```

```python
import jax
import jax.numpy as jnp
from jax import lax
from jax.experimental import pallas as pl
from jax.experimental.pallas import tpu as pltpu
from jax.sharding import PartitionSpec as P

EPSILON = 1e-05
MESH = pl.DeviceIdType.MESH
F32 = jnp.float32
BF16 = jnp.bfloat16

D = 1024
HALF = 512
CH = 256
CB = 64
FQ = 1152
FB = 288
TC = 256
TO = 64
COPIES = 256


def mod4(value):
    return lax.rem(value + 4, 4)


def nt(a, b):
    return lax.dot_general(a, b, (((1,), (1,)), ((), ())), preferred_element_type=F32)


def nn(a, b):
    return lax.dot_general(a, b, (((1,), (0,)), ((), ())), preferred_element_type=F32)


def tn(a, b):
    return lax.dot_general(a, b, (((0,), (0,)), ((), ())), preferred_element_type=F32)


def loop(count, body):
    def step(i, carry):
        body(i)
        return carry

    lax.fori_loop(0, count, step, 0)


def rows_at(start, size, multiple=32):
    return pl.ds(pl.multiple_of(start, multiple), size)


def lanes_at(start, size):
    return pl.ds(pl.multiple_of(start, 128), size)


def kernel(
    x_in,
    cot_in,
    ids,
    first_in,
    second_in,
    taps_own,
    b_in,
    c_in,
    v_in,
    out_in,
    gate_in,
    up_in,
    down_in,
    block_o,
    input_o,
    mix_o,
    feed_o,
    stats_o,
    small,
    masks,
    xs,
    cs,
    gains,
    taps_in,
    w_mix,
    w_feed,
    fn,
    pre,
    gat,
    cvd,
    mx,
    res,
    sn,
    gu,
    hid,
    dg,
    fulls,
    halves,
    recvs,
    rg,
    rh,
    cg,
    dm,
    go_f,
    cr_f,
    s_f,
    zr_f,
    xs_f,
    xr_f,
    xf_f,
    x1_d,
    t_d,
    z2_d,
    go_m,
    cr_m,
    s_m,
    zr_m,
    xs_m,
    xr_m,
    xf_m,
    st,
    st_y,
    st_z,
    st_x,
    bo_own,
    ig_own,
    ss,
    rs,
    ls,
):
    x = lax.axis_index("dp")
    r = lax.axis_index("row")
    col = lax.axis_index("col")
    z = lax.div(col, 4)
    y = lax.rem(col, 4)
    other = 1 - r
    own_lanes = lanes_at(r * HALF, HALF)
    other_lanes = lanes_at(other * HALF, HALF)
    own_rows = rows_at(y * TO, TO)

    def y_peer(d):
        return (x, r, z * 4 + mod4(y + d))

    def z_peer(d):
        return (x, r, mod4(z + d) * 4 + y)

    def x_peer(d):
        return (mod4(x + d), r, col)

    partner = (x, other, col)
    successor = (x, other, mod4(z + r) * 4 + y)
    predecessor = (x, other, mod4(z + r + 3) * 4 + y)
    halo_extra = (x, other, mod4(z + 2 * r - 1) * 4 + y)

    barrier = pltpu.get_barrier_semaphore()
    greeted = [partner, halo_extra]
    for d in (1, 2, 3):
        greeted += [y_peer(d), (x, other, z * 4 + mod4(y + d)), z_peer(d), x_peer(d)]
    for device in greeted:
        pl.semaphore_signal(barrier, inc=1, device_id=device, device_id_type=MESH)
    pl.semaphore_wait(barrier, len(greeted))

    used = [0]
    sent = []

    def slot(count=1):
        first = used[0]
        used[0] += count
        return first

    def push(source, target, device, index=None):
        i = slot() if index is None else index
        copy = pltpu.make_async_remote_copy(
            src_ref=source,
            dst_ref=target,
            send_sem=ss.at[i],
            recv_sem=rs.at[i],
            device_id=device,
            device_id_type=MESH,
        )
        copy.start()
        sent.append((None, copy))
        return copy

    def place(source, target, device, send_index, recv_index, here):
        copy = pltpu.make_async_remote_copy(
            src_ref=source,
            dst_ref=target,
            send_sem=ss.at[send_index],
            recv_sem=rs.at[recv_index],
            device_id=device,
            device_id_type=MESH,
        )

        @pl.when(here)
        def _():
            pltpu.make_async_copy(source, target, rs.at[recv_index]).start()

        @pl.when(jnp.logical_not(here))
        def _():
            copy.start()

        sent.append((here, copy))

    def arrived(source, target, index):
        pltpu.make_async_remote_copy(
            src_ref=source,
            dst_ref=target,
            send_sem=ss.at[index],
            recv_sem=rs.at[index],
            device_id=partner,
            device_id_type=MESH,
        ).wait_recv()

    def tokens_start(source, target):
        base = slot(4)
        core = lax.div(y, 2)
        block = lax.rem(y, 2)
        region = target.at[rows_at(block * 128, 128), own_lanes]
        for d in (1, 3, 2, 0):
            device = (x, core, z * 4 + mod4(y + d))
            index = base + block * 2 + r
            if d:
                copy = pltpu.make_async_remote_copy(
                    src_ref=source,
                    dst_ref=region,
                    send_sem=ss.at[base + d],
                    recv_sem=rs.at[index],
                    device_id=device,
                    device_id_type=MESH,
                )
                copy.start()
                sent.append((None, copy))
            else:
                place(source, region, device, base, index, core == r)
        return base

    def tokens_finish(source, target, base):
        for s in range(4):
            region = target.at[pl.ds((s // 2) * 128, 128), pl.ds((s % 2) * HALF, HALF)]
            arrived(source, region, base + s)

    def owners_start(source, target):
        base = slot(2)
        chip = 2 * r + lax.div(y, 2)
        region = target.at[rows_at(lax.rem(y, 2) * TO, TO)]
        for core in range(2):
            here = jnp.logical_and(chip == y, r == core)
            place(
                source.at[:, pl.ds(core * HALF, HALF)],
                region,
                (x, core, z * 4 + chip),
                base + core,
                base + lax.rem(y, 2),
                here,
            )
        return base

    def owners_finish(source, target, base):
        for s in range(2):
            arrived(source.at[:, pl.ds(0, HALF)], target.at[pl.ds(s * TO, TO)], base + s)

    local = [0]

    class Section:
        def __init__(self, source, region):
            self.source = source
            self.region = region

        def start(self):
            self.z = {d: push(self.source, self.region(z, r), z_peer(d)) for d in (1, 3, 2)}
            self.mine = pltpu.make_async_copy(self.source, self.region(z, r), ls.at[local[0]])
            local[0] += 1
            self.mine.start()
            self.cross = [push(self.source, self.region(z, r), partner)]

        def forward(self):
            for d in (1, 3, 2):
                self.z[d].wait_recv()
                region = self.region(mod4(z - d), r)
                self.cross.append(push(region, region, partner))

        def finish(self):
            self.mine.wait()
            for copy in self.cross:
                copy.wait_recv()

    class Split:
        def __init__(self, source, region):
            self.source = source
            self.region = region

        def start(self):
            quarter = self.source.at[:, lanes_at(x * 128, 128)]
            self.z = {
                d: push(quarter, self.region(z, r * HALF + x * 128, 128), z_peer(d))
                for d in (1, 3, 2)
            }
            whole = self.region(z, r * HALF, HALF)
            self.mine = pltpu.make_async_copy(self.source, whole, ls.at[local[0]])
            local[0] += 1
            self.mine.start()
            self.cross = [push(self.source, whole, partner)]

        def forward(self):
            self.x = []
            for d in (1, 3, 2):
                self.z[d].wait_recv()
                region = self.region(mod4(z - d), r * HALF + x * 128, 128)
                self.x += [push(region, region, x_peer(e)) for e in (1, 3, 2)]

        def across(self):
            for copy in self.x:
                copy.wait_recv()
            for d in (1, 3, 2):
                region = self.region(mod4(z - d), r * HALF, HALF)
                self.cross.append(push(region, region, partner))

        def finish(self):
            self.mine.wait()
            for copy in self.cross:
                copy.wait_recv()

    def mix_section(s, source):
        return Section(
            source, lambda zz, rr: w_mix.at[s, rows_at(zz * CB, CB), lanes_at(rr * HALF, HALF)]
        )

    mix = [mix_section(s, source) for s, source in enumerate((b_in, c_in, v_in, out_in))]
    gate = Section(
        gate_in, lambda zz, rr: w_feed.at[rows_at(zz * FB, FB), lanes_at(rr * HALF, HALF)]
    )
    up = Split(
        up_in, lambda zz, at, size: w_feed.at[rows_at(FQ + zz * FB, FB), lanes_at(at, size)]
    )
    down = Split(
        down_in,
        lambda zz, at, size: w_feed.at[rows_at(2 * FQ + zz * FB, FB), lanes_at(at, size)],
    )

    def scatter_start(k):
        return [
            push(halves.at[k, rows_at(mod4(y + d) * TO, TO)], recvs.at[k, d - 1], y_peer(d))
            for d in (1, 3, 2)
        ]

    def scatter_finish(k, copies):
        for copy in copies:
            copy.wait_recv()
        total = fulls[k, own_rows, :]
        for d in range(3):
            total = total + recvs[k, d].astype(F32)
        return total

    def gather_start(buffer):
        return [push(buffer.at[own_rows], buffer.at[own_rows], y_peer(d)) for d in (1, 3, 2)]

    def wait(copies):
        for copy in copies:
            copy.wait_recv()

    def product(k, value):
        def body(n):
            lanes = lanes_at(n * 256, 256)
            part = value(lanes)
            fulls[k, :, lanes] = part
            halves[k, :, lanes] = part.astype(BF16)

        loop(4, body)

    small[0:1, :] = first_in[...]
    small[1:2, :] = second_in[...]
    small[2:5, 0:CH] = taps_own[...]
    x_base = tokens_start(x_in, xs)
    for section in mix:
        section.start()
    small_copies = [push(small, gains.at[:, own_lanes], partner)]
    small_copies += [push(small, taps_in.at[d - 1], z_peer(d)) for d in (1, 3, 2)]
    gains[:, own_lanes] = small[...]
    st[...] = jnp.zeros((8, D), F32)
    here = ids[2 : 2 + TC, :]
    for k, first in enumerate((1, 0, 3, 4)):
        masks[k] = (ids[first : first + TC, :] == here).astype(F32)

    tokens_finish(x_in, xs, x_base)
    wait(small_copies)
    cot_base = tokens_start(cot_in, cs)
    first_gain = gains[0:1, :]
    second_gain = gains[1:2, :]
    taps = small[2:5, 0:CH]
    for d in range(3):
        taps = taps + taps_in[d, 2:5, 0:CH]

    def norm_body(i):
        rows = rows_at(i * 32, 32)
        value = xs[rows, :].astype(F32)
        scale = lax.rsqrt(jnp.sum(value * value, axis=1, keepdims=True) / D + EPSILON)
        fn[rows, :] = (value * scale * first_gain).astype(BF16)

    loop(8, norm_body)

    for section in mix:
        section.forward()
    for section in mix:
        section.finish()

    def pre_body(s):
        pre[s] = nt(fn[...], w_mix[s])

    loop(3, pre_body)

    gat[8 : 8 + TC, :] = pre[0] * pre[2]
    halo = push(gat.at[pl.ds(TC, 8)], gat.at[pl.ds(0, 8)], successor)
    halo.wait_recv()
    up.start()
    down.start()
    gate.start()
    m1 = masks[0, :, 0:1]
    m2 = masks[1, :, 0:1]
    cvd[...] = (
        taps[0:1] * gat[8 : 8 + TC, :]
        + taps[1:2] * (m1 * gat[7 : 7 + TC, :])
        + taps[2:3] * (m2 * gat[6 : 6 + TC, :])
    )
    mx[...] = (pre[1] * cvd[...]).astype(BF16)
    product(0, lambda lanes: nn(mx[...], w_mix[3, :, lanes]))
    first_scatter = scatter_start(0)
    up.forward()
    down.forward()

    residual = xs[own_rows, :].astype(F32) + scatter_finish(0, first_scatter)
    res[...] = residual
    second_scale = lax.rsqrt(jnp.sum(residual * residual, axis=1, keepdims=True) / D + EPSILON)
    sn[own_rows, :] = (residual * second_scale * second_gain).astype(BF16)
    sn_copies = gather_start(sn)

    gate.forward()
    up.across()
    tokens_finish(cot_in, cs, cot_base)
    gate.finish()
    up.finish()
    wait(sn_copies)

    def gu_body(n):
        at = n * 256
        gu[:, lanes_at(at, 256)] = nt(sn[...], w_feed[rows_at(at, 256), :])

    loop(9, gu_body)

    down.across()

    def hidden_body(i):
        rows = rows_at(i * 32, 32)
        g = gu[rows, 0:FQ]
        hid[rows, :] = (g * jax.nn.sigmoid(g) * gu[rows, FQ : 2 * FQ]).astype(BF16)

    loop(8, hidden_body)
    down.finish()

    def hg_body(n):
        at = n * 384
        gu[:, lanes_at(2 * FQ + at, 384)] = nt(cs[...], w_feed[rows_at(2 * FQ + at, 384), :])

    loop(3, hg_body)

    def delta_body(i):
        rows = rows_at(i * 32, 32)
        g = gu[rows, 0:FQ]
        u = gu[rows, FQ : 2 * FQ]
        hg = gu[rows, 2 * FQ : 3 * FQ]
        s = jax.nn.sigmoid(g)
        dg[rows, 0:FQ] = (hg * u * s * (1.0 + g * (1.0 - s))).astype(BF16)
        dg[rows, FQ : 2 * FQ] = (hg * (g * s)).astype(BF16)

    loop(8, delta_body)
    product(2, lambda lanes: nn(dg[...], w_feed[0 : 2 * FQ, lanes]))
    grad_scatter = scatter_start(2)
    def go_gu_body(n):
        at = n * 384
        go_f[rows_at(at, 384), :] = tn(dg[:, lanes_at(at, 384)], sn[:, other_lanes]).astype(BF16)

    def go_d_body(n):
        at = n * 384
        go_f[rows_at(2 * FQ + at, 384), :] = tn(
            hid[:, lanes_at(at, 384)], cs[:, other_lanes]
        ).astype(BF16)

    loop(6, go_gu_body)
    cross_gu = push(go_f.at[pl.ds(0, 2 * FQ)], cr_f.at[pl.ds(0, 2 * FQ)], partner)
    loop(3, go_d_body)
    cross_d = push(go_f.at[pl.ds(2 * FQ, FQ)], cr_f.at[pl.ds(2 * FQ, FQ)], partner)

    cross_gu.wait_recv()

    def s_gu_body(n):
        at = n * 384
        rows = rows_at(at, 384)
        s_f[rows, :] = (
            tn(dg[:, lanes_at(at, 384)], sn[:, own_lanes]) + cr_f[rows, :].astype(F32)
        ).astype(BF16)

    loop(6, s_gu_body)

    def feed_send(part):
        return [
            push(
                s_f.at[rows_at(part * FQ + mod4(z + d) * FB, FB)],
                zr_f.at[d - 1, pl.ds(part * FB, FB)],
                z_peer(d),
            )
            for d in (1, 3, 2)
        ]

    feed_z = feed_send(0)
    second_grad = scatter_finish(2, grad_scatter)
    residual = res[...]
    second_scale = lax.rsqrt(jnp.sum(residual * residual, axis=1, keepdims=True) / D + EPSILON)
    st[1:2, :] = jnp.sum(second_grad * residual * second_scale, axis=0, keepdims=True)
    weighted = second_grad * second_gain
    cube = second_scale * second_scale * second_scale
    residual_grad = (
        cs[own_rows, :].astype(F32)
        + second_scale * weighted
        - residual * cube * (jnp.sum(weighted * residual, axis=1, keepdims=True) / D)
    )
    rg[...] = residual_grad
    rh[own_rows, :] = residual_grad.astype(BF16)
    rh_copies = gather_start(rh)

    cross_d.wait_recv()

    def s_d_body(n):
        at = n * 384
        rows = rows_at(2 * FQ + at, 384)
        s_f[rows, :] = (
            tn(hid[:, lanes_at(at, 384)], cs[:, own_lanes]) + cr_f[rows, :].astype(F32)
        ).astype(BF16)

    loop(3, s_d_body)
    down_x = [
        push(s_f.at[pl.ds(2 * FQ, FQ), lanes_at(mod4(x + d) * 128, 128)], x1_d.at[d - 1], x_peer(d))
        for d in (1, 3, 2)
    ]
    product(1, lambda lanes: nn(hid[...], w_feed[2 * FQ : 3 * FQ, lanes]))
    block_scatter = scatter_start(1)

    wait(rh_copies)
    mixed_grad = nt(rh[...], w_mix[3])
    cg[0:TC, :] = mixed_grad * pre[1]
    halo_back = push(cg.at[pl.ds(0, 8)], cg.at[pl.ds(TC, 8)], predecessor)
    dm[1] = (mixed_grad * cvd[...]).astype(BF16)

    go_m[3] = tn(mx[...], rh[:, other_lanes]).astype(BF16)

    conv_grad = cg[0:TC, :]
    tap_lanes = lanes_at(y * CH, CH)
    st[2:3, tap_lanes] = jnp.sum(conv_grad * gat[8 : 8 + TC, :], axis=0, keepdims=True)
    st[3:4, tap_lanes] = jnp.sum(conv_grad * m1 * gat[7 : 7 + TC, :], axis=0, keepdims=True)
    st[4:5, tap_lanes] = jnp.sum(conv_grad * m2 * gat[6 : 6 + TC, :], axis=0, keepdims=True)
    halo_back.wait_recv()
    feed_z += feed_send(1)
    gated_grad = (
        taps[0:1] * conv_grad
        + taps[1:2] * (masks[2, :, 0:1] * cg[1 : 1 + TC, :])
        + taps[2:3] * (masks[3, :, 0:1] * cg[2 : 2 + TC, :])
    )
    dm[0] = (gated_grad * pre[2]).astype(BF16)
    dm[2] = (gated_grad * pre[0]).astype(BF16)

    def first_part(lanes):
        part = nn(dm[0], w_mix[0, :, lanes])
        part = part + nn(dm[1], w_mix[1, :, lanes])
        return part + nn(dm[2], w_mix[2, :, lanes])

    product(3, first_part)
    first_scatter = scatter_start(3)

    def go_m_body(s):
        go_m[s] = tn(dm[s], fn[:, other_lanes]).astype(BF16)

    loop(3, go_m_body)
    cross_m = push(go_m, cr_m, partner)

    x_lanes = lanes_at(x * 128, 128)
    wait(down_x)
    mine = s_f[2 * FQ : 3 * FQ, x_lanes].astype(F32)
    for d in range(3):
        mine = mine + x1_d[d].astype(F32)
    t_d[...] = mine.astype(BF16)
    down_z = [
        push(t_d.at[rows_at(mod4(z + d) * FB, FB)], z2_d.at[d - 1], z_peer(d)) for d in (1, 3, 2)
    ]

    cross_m.wait_recv()

    def s_m_body(s):
        s_m[s] = (tn(dm[s], fn[:, own_lanes]) + cr_m[s].astype(F32)).astype(BF16)

    loop(3, s_m_body)
    s_m[3] = (tn(mx[...], rh[:, own_lanes]) + cr_m[3].astype(F32)).astype(BF16)
    mix_z = [
        push(s_m.at[:, rows_at(mod4(z + d) * CB, CB), :], zr_m.at[d - 1], z_peer(d))
        for d in (1, 3, 2)
    ]

    wait(feed_z)
    for part in range(2):
        mine = s_f[rows_at(part * FQ + z * FB, FB), :].astype(F32)
        at = part * FB
        for d in range(3):
            mine = mine + zr_f[d, at : at + FB, :].astype(F32)
        xs_f[at : at + FB, :] = mine.astype(BF16)
    feed_x = [
        push(xs_f.at[:, lanes_at(mod4(x + d) * 128, 128)], xr_f.at[d - 1], x_peer(d))
        for d in (1, 3, 2)
    ]

    kept = []

    def spread(source, target):
        copy = pltpu.make_async_copy(source, target, ls.at[local[0]])
        local[0] += 1
        copy.start()
        kept.append(copy)
        return [push(source, target, x_peer(d)) for d in (1, 3, 2)]

    wait(down_z)
    mine = t_d[rows_at(z * FB, FB), :].astype(F32)
    for d in range(3):
        mine = mine + z2_d[d].astype(F32)
    xf_f[2 * FB : 3 * FB, :] = mine.astype(BF16)
    down_rows = pl.ds(2 * FB, FB)
    feed_g = spread(xf_f.at[down_rows], feed_o.at[down_rows, x_lanes])

    bo_own[...] = (res[...] + scatter_finish(1, block_scatter)).astype(BF16)
    bo_base = owners_start(bo_own, block_o)

    first_grad = scatter_finish(3, first_scatter)
    value = xs[own_rows, :].astype(F32)
    first_scale = lax.rsqrt(jnp.sum(value * value, axis=1, keepdims=True) / D + EPSILON)
    st[0:1, :] = jnp.sum(first_grad * value * first_scale, axis=0, keepdims=True)
    weighted = first_grad * first_gain
    cube = first_scale * first_scale * first_scale
    ig_own[...] = (
        rg[...]
        + first_scale * weighted
        - value * cube * (jnp.sum(weighted * value, axis=1, keepdims=True) / D)
    )
    ig_base = owners_start(ig_own, input_o)
    stat_copies = [push(st, st_y.at[0], partner)]
    for d in (1, 2, 3):
        stat_copies.append(push(st, st_y.at[2 * d - 1], y_peer(d)))
        stat_copies.append(push(st, st_y.at[2 * d], (x, other, z * 4 + mod4(y + d))))

    wait(feed_x)
    mine = xs_f[:, x_lanes].astype(F32)
    for d in range(3):
        mine = mine + xr_f[d].astype(F32)
    xf_f[0 : 2 * FB, :] = mine.astype(BF16)
    gate_rows = pl.ds(0, 2 * FB)
    feed_g += spread(xf_f.at[gate_rows], feed_o.at[gate_rows, x_lanes])

    wait(stat_copies)
    total = st[...]
    for i in range(7):
        total = total + st_y[i]
    st_z[3] = total
    stat_copies = [push(st_z.at[3], st_z.at[d - 1], z_peer(d)) for d in (1, 3, 2)]

    wait(mix_z)
    mine = s_m[:, rows_at(z * CB, CB), :].astype(F32)
    for d in range(3):
        mine = mine + zr_m[d].astype(F32)
    xs_m[...] = mine.astype(BF16)
    mix_x = [
        push(xs_m.at[:, :, lanes_at(mod4(x + d) * 128, 128)], xr_m.at[d - 1], x_peer(d))
        for d in (1, 3, 2)
    ]
    wait(stat_copies)
    st_x[3] = st_z[0] + st_z[1] + st_z[2] + st_z[3]
    stat_copies = [push(st_x.at[3], st_x.at[d - 1], x_peer(d)) for d in (1, 3, 2)]

    wait(mix_x)
    mine = xs_m[:, :, x_lanes].astype(F32)
    for d in range(3):
        mine = mine + xr_m[d].astype(F32)
    xf_m[...] = mine.astype(BF16)
    mix_g = spread(xf_m, mix_o.at[:, :, x_lanes])

    wait(stat_copies)
    stats_o[...] = st_x[0] + st_x[1] + st_x[2] + st_x[3]
    owners_finish(bo_own, block_o, bo_base)
    owners_finish(ig_own, input_o, ig_base)
    wait(feed_g)
    wait(mix_g)
    for copy in kept:
        copy.wait()

    for here, copy in sent:
        if here is None:
            copy.wait_send()
        else:

            @pl.when(jnp.logical_not(here))
            def _(copy=copy):
                copy.wait_send()


def finish(
    block_i,
    input_i,
    mix_i,
    feed_i,
    stats,
    block_o,
    input_o,
    b_o,
    c_o,
    v_o,
    out_o,
    gate_o,
    up_o,
    down_o,
    first_o,
    second_o,
    taps_o,
):
    r = lax.axis_index("row")
    col = lax.axis_index("col")
    z = lax.div(col, 4)
    y = lax.rem(col, 4)
    block_o[...] = block_i[...]
    input_o[...] = input_i[...]
    lanes = lanes_at(r * HALF, HALF)
    first_o[...] = stats[0:1, lanes]
    second_o[...] = stats[1:2, lanes]
    window = stats[2:5, lanes_at(y * CH + lax.div(z, 2) * 128, 128)]
    place = lax.rem(z, 2) * 2 + r
    total = jnp.zeros((3, 32), F32)
    for k in range(4):
        total = total + jnp.where(place == k, window[:, k * 32 : (k + 1) * 32], 0.0)
    taps_o[...] = total
    for part, target in enumerate((gate_o, up_o, down_o)):
        target[...] = feed_i[part * FB : (part + 1) * FB, :].astype(F32)
    for part, target in enumerate((b_o, c_o, v_o, out_o)):
        target[...] = mix_i[part].astype(F32)


def shards(
    hidden_in,
    segment_ids,
    first_gain,
    mixer_b,
    mixer_c,
    mixer_v,
    conv_kernel,
    mixer_out,
    second_gain,
    gate_weight,
    up_weight,
    down_weight,
    cotangent,
):
    r = lax.axis_index("row")
    col = lax.axis_index("col")
    z = col // 4
    y = col % 4
    ids = jnp.pad(segment_ids[0], ((2, 6),), constant_values=-1)
    ids = lax.dynamic_slice_in_dim(ids, z * 512 + r * TC, TC + 8, 0)
    ids = jnp.broadcast_to(ids[:, None], (TC + 8, 128))
    at_z = lax.broadcasted_iota(jnp.int32, (3, CH), 1) // CB == z
    taps = jnp.where(at_z, jnp.tile(conv_kernel, (1, CH // CB)), 0.0)
    vmem = pl.BlockSpec(memory_space=pltpu.VMEM)
    whole = pl.BlockSpec(memory_space=pl.ANY)
    shape = jax.ShapeDtypeStruct
    scratch = [
        ((8, HALF), F32),
        ((4, TC, 128), F32),
        ((TC, D), BF16),
        ((TC, D), BF16),
        ((8, D), F32),
        ((3, 8, HALF), F32),
        ((4, CH, D), BF16),
        ((3 * FQ, D), BF16),
        ((TC, D), BF16),
        ((3, TC, CH), F32),
        ((TC + 8, CH), F32),
        ((TC, CH), F32),
        ((TC, CH), BF16),
        ((TO, D), F32),
        ((TC, D), BF16),
        ((TC, 3 * FQ), F32),
        ((TC, FQ), BF16),
        ((TC, 2 * FQ), BF16),
        ((4, TC, D), F32),
        ((4, TC, D), BF16),
        ((4, 3, TO, D), BF16),
        ((TO, D), F32),
        ((TC, D), BF16),
        ((TC + 8, CH), F32),
        ((3, TC, CH), BF16),
        ((3 * FQ, HALF), BF16),
        ((3 * FQ, HALF), BF16),
        ((3 * FQ, HALF), BF16),
        ((3, 2 * FB, HALF), BF16),
        ((2 * FB, HALF), BF16),
        ((3, 2 * FB, 128), BF16),
        ((3 * FB, 128), BF16),
        ((3, FQ, 128), BF16),
        ((FQ, 128), BF16),
        ((3, FB, 128), BF16),
        ((4, CH, HALF), BF16),
        ((4, CH, HALF), BF16),
        ((4, CH, HALF), BF16),
        ((3, 4, CB, HALF), BF16),
        ((4, CB, HALF), BF16),
        ((3, 4, CB, 128), BF16),
        ((4, CB, 128), BF16),
        ((8, D), F32),
        ((7, 8, D), F32),
        ((4, 8, D), F32),
        ((4, 8, D), F32),
        ((TO, D), BF16),
        ((TO, D), F32),
    ]
    results = pl.pallas_call(
        kernel,
        out_shape=(
            shape((128, HALF), BF16),
            shape((128, HALF), F32),
            shape((4, CB, HALF), BF16),
            shape((3 * FB, HALF), BF16),
            shape((8, D), F32),
        ),
        in_specs=[whole] * 2 + [vmem] * 4 + [whole] * 7,
        out_specs=(whole,) * 4 + (vmem,),
        scratch_shapes=[pltpu.VMEM(s, t) for s, t in scratch]
        + [
            pltpu.SemaphoreType.DMA((COPIES,)),
            pltpu.SemaphoreType.DMA((COPIES,)),
            pltpu.SemaphoreType.DMA((10,)),
        ],
        compiler_params=pltpu.CompilerParams(
            collective_id=0, has_side_effects=True, vmem_limit_bytes=62 * 2**20
        ),
    )(
        hidden_in,
        cotangent,
        ids,
        first_gain[None],
        second_gain[None],
        taps,
        mixer_b.T,
        mixer_c.T,
        mixer_v.T,
        mixer_out,
        gate_weight.T,
        up_weight.T,
        down_weight,
    )
    copied = [((128, HALF), BF16), ((128, HALF), F32)]
    small_out = [((1, HALF), F32), ((1, HALF), F32), ((3, 32), F32)]
    grads = [((CB, HALF), F32)] * 4 + [((FB, HALF), F32)] * 3
    outs = pl.pallas_call(
        finish,
        out_shape=tuple(shape(a, t) for a, t in copied + grads + small_out),
        in_specs=[vmem] * 5,
        out_specs=(vmem,) * 12,
    )(*results)
    block_out, input_grad, b_g, c_g, v_g, out_g, gate_g, up_g, down_g, first_g, second_g, taps_g = outs
    return (
        block_out,
        input_grad,
        first_g[0],
        b_g.T,
        c_g.T,
        v_g.T,
        taps_g,
        out_g,
        second_g[0],
        gate_g.T,
        up_g.T,
        down_g,
    )


def solution(mesh):
    return jax.shard_map(
        shards,
        mesh=mesh,
        in_specs=(
            P(("dp", "col"), "row"),
            P("dp", None),
            P("row"),
            P("row", "col"),
            P("row", "col"),
            P("row", "col"),
            P(None, "col"),
            P("col", "row"),
            P("row"),
            P("row", "col"),
            P("row", "col"),
            P("col", "row"),
            P(("dp", "col"), "row"),
        ),
        out_specs=(
            P(("dp", "col"), "row"),
            P(("dp", "col"), "row"),
            P("row"),
            P("row", "col"),
            P("row", "col"),
            P("row", "col"),
            P(None, ("col", "row")),
            P("col", "row"),
            P("row"),
            P("row", "col"),
            P("row", "col"),
            P("col", "row"),
        ),
        check_vma=False,
    )
```
